32 devices in a mesh: ctx: 8 (over z, x), inner: 4 (over y, core).
Axes of the slice: x: 2, y: 2, z: 4, core: 2. Of those that a mesh axis runs over, the one named last changes fastest.
Arguments:
- lin_query: bfloat16 [4096, 4096], P(('ctx', 'inner')), may hold values from -6 to 6
- lin_key: bfloat16 [4096, 4096], P(('ctx', 'inner')), may hold values from -6 to 6
- lin_value: bfloat16 [4096, 4096], P(('ctx', 'inner')), may hold values from -6 to 6
- sparse_query: bfloat16 [4096, 4096], P(('ctx', 'inner')), may hold values from -48 to 48
- sparse_key: bfloat16 [4096, 4096], P(('ctx', 'inner')), may hold values from -48 to 48
- decay: float32 [32, 4096], P('inner', 'ctx'), may hold values from 0.5 to 1
- norm_gain: float32 [32, 128], P('inner'), may hold values from 0.1 to 1.9
- block_pattern: int32 [64, 8], P('ctx'), may hold values from -1 to 63, as said below
Outputs:
- layer_out: bfloat16 [4096, 4096], P(('ctx', 'inner'))
The draws below stay inside these ranges and needn't reach their ends.
Inputs may be any that keep to these rules, and one draw needn't show every extreme that they name: `block_pattern`: row i lists distinct blocks: the first entry is i, the others lie in i - 16 to i - 1, and -1 stands where that range falls before block 0; in a row whose index is a multiple of 8 the last entry is i - 16.
All inputs are finite; a program needn't handle non-finite values.
Results may differ from the reference program's by a relative error of at most 0.0049.
Values may be sent and summed in bfloat16 or wider, within the bound.
No kernel may reach another device: no remote copies, remote signals or barrier semaphores. Data moves between devices by JAX's collectives and lax.ppermute only.
A program may use at most 128 MiB of HBM per device.

```python
import math
import jax
import jax.numpy as jnp
from jax import lax

H = 32
HD = 128
D = 4096
LBLK = 128
BLK = 64
NSEL = 8
TOKEN_COUNT = 4096
SHARD_BLOCKS = 8
WIN_B = 16
QB = 64


def draw_decay(key, part):
    quick_random_key, span_random_key, gradual_random_key, noise_random_key, spike_random_key, retain_random_key = jax.random.split(jax.random.fold_in(key, 11), 6)
    fast_count = 5
    is_fast = jax.random.randint(quick_random_key, (H, 1), 0, 10) < fast_count
    fast_rate = 1.0 / jax.random.uniform(span_random_key, (H, 1), minval=30.0, maxval=50.0)
    slow_rate = math.log(2.0) * jax.random.uniform(gradual_random_key, (H, 1), minval=0.2, maxval=0.8) / TOKEN_COUNT
    baseline_decay_rate = jnp.where(is_fast, fast_rate, slow_rate)
    noise_jitter = jnp.exp(jax.random.uniform(noise_random_key, (H, TOKEN_COUNT), minval=-math.log(2.0), maxval=math.log(2.0)))
    spike_position = jax.random.randint(spike_random_key, (2,), 0, TOKEN_COUNT)
    inside_spike = jnp.any(jnp.arange(TOKEN_COUNT)[None, :] == spike_position[:, None], axis=0)
    retained_fraction = jax.random.uniform(retain_random_key, (H, 1), minval=0.6, maxval=0.8)
    return (jnp.exp(-baseline_decay_rate * noise_jitter) * jnp.where(inside_spike[None, :], retained_fraction, 1.0)).astype(jnp.float32)


def sparse_pair(key):
    key_query, key_keys = jax.random.split(jax.random.fold_in(key, 29), 2)
    queries = jnp.clip(jax.random.normal(key_query, (TOKEN_COUNT, D)), -6.0, 6.0)
    keys_all = jnp.clip(jax.random.normal(key_keys, (TOKEN_COUNT, D)), -6.0, 6.0)
    return (queries, keys_all)


def draw_sparse_query(key, part):
    return sparse_pair(key)[0].astype(jnp.bfloat16)


def draw_sparse_key(key, part):
    return sparse_pair(key)[1].astype(jnp.bfloat16)


def draw_block_pattern(key, part):
    row_keys = jax.random.split(jax.random.fold_in(key, 5), QB)
    offsets_all = jax.vmap(lambda row_key: jax.random.permutation(row_key, WIN_B - 1))(row_keys).astype(jnp.int32) + 1
    rows = jnp.arange(QB, dtype=jnp.int32)
    opens_shard = rows % SHARD_BLOCKS == 0
    last_offset = jnp.where(opens_shard, WIN_B, offsets_all[:, NSEL - 2]).astype(jnp.int32)
    chosen_offsets = jnp.concatenate([jnp.zeros((QB, 1), jnp.int32), offsets_all[:, :NSEL - 2], last_offset[:, None]], axis=1)
    blocks = rows[:, None] - chosen_offsets
    return jnp.where(blocks >= 0, blocks, -1).astype(jnp.int32)


def shard_levels(rng, extent, shards, low, high):
    loudness = 1.0
    for position, blocks in shards:
        draws = jax.random.uniform(jax.random.fold_in(jax.random.fold_in(rng, 6), position), (blocks,), jnp.float32, low / len(shards), high / len(shards))
        loudness = loudness * jnp.repeat(jnp.exp(draws), extent[position] // blocks).reshape((-1,) + (1,) * (len(extent) - 1 - position))
    return loudness


def gaussian(key, shape, width, limit, pieces=(), kind=jnp.bfloat16):
    result = width * jax.random.normal(key, shape, jnp.float32)
    if pieces:
        result = result * shard_levels(key, shape, pieces, -0.22, 0.18)
    return jnp.clip(result, -limit, limit).astype(kind)


def setup_inputs(seed: int = 0) -> dict:
    arg_keys = jax.random.split(jax.random.key(seed), 9)
    return {
        "lin_query": gaussian(arg_keys[0], (TOKEN_COUNT, D), 1.0, 6.0, ((0, 32),)),
        "lin_key": gaussian(arg_keys[1], (TOKEN_COUNT, D), 1.0, 6.0, ((0, 32),)),
        "lin_value": gaussian(arg_keys[2], (TOKEN_COUNT, D), 1.0, 6.0, ((0, 32),)),
        "sparse_query": draw_sparse_query(jax.random.fold_in(arg_keys[8], 71), 0),
        "sparse_key": draw_sparse_key(jax.random.fold_in(arg_keys[8], 71), 0),
        "decay": draw_decay(jax.random.fold_in(arg_keys[8], 71), 0),
        "norm_gain": jnp.clip(1.0 + 0.18 * jax.random.normal(arg_keys[6], (H, HD), jnp.float32), 0.1, 1.9),
        "block_pattern": draw_block_pattern(jax.random.fold_in(arg_keys[8], 71), 0),
    }


precise_mode = lax.Precision.HIGHEST

def block_math(queries_blk, keys_blk, values_blk, cumul, carried):
    query_f = queries_blk.astype(jnp.float32)
    key_f = keys_blk.astype(jnp.float32)
    value_f = values_blk.astype(jnp.float32)
    scores = jnp.einsum('ihd,jhd->hij', query_f, key_f, precision=precise_mode)
    length = cumul.shape[1]
    causal = (jnp.arange(length)[:, None] >= jnp.arange(length)[None, :])[None]
    log_gap = cumul[:, :, None] - cumul[:, None, :]
    weights = jnp.where(causal, jnp.exp(jnp.where(causal, log_gap, 0.0)), 0.0) * scores
    inside = jnp.einsum('hij,jhd->ihd', weights, value_f, precision=precise_mode)
    lifted = query_f * jnp.exp(cumul).T[:, :, None]
    outside = jnp.einsum('ihd,hde->ihe', lifted, carried, precision=precise_mode)
    final_log = cumul[:, -1]
    tail_scale = jnp.exp(final_log[:, None] - cumul).T[:, :, None]
    new_state = jnp.exp(final_log)[:, None, None] * carried + jnp.einsum('jhd,jhe->hde', key_f * tail_scale, value_f, precision=precise_mode)
    return (inside + outside, new_state)

def normalize(raw_out, norm_gain):
    scale_rows = lax.rsqrt(lax.optimization_barrier(jnp.mean(raw_out * raw_out, axis=-1, keepdims=True)) + 1e-06)
    return (raw_out * scale_rows * norm_gain).astype(jnp.bfloat16)

def reference(lin_query, lin_key, lin_value, sparse_query, sparse_key, decay, norm_gain, block_pattern):
    num_blocks = TOKEN_COUNT // LBLK
    query_blocks = lin_query.reshape(num_blocks, LBLK, H, HD)
    key_blocks = lin_key.reshape(num_blocks, LBLK, H, HD)
    value_blocks = lin_value.reshape(num_blocks, LBLK, H, HD)
    block_logs = jnp.log(decay).reshape(H, num_blocks, LBLK).transpose(1, 0, 2)

    def advance(carried, inputs):
        queries_blk, keys_blk, values_blk, logs_blk = inputs
        produced, carried = block_math(queries_blk, keys_blk, values_blk, jnp.cumsum(logs_blk, axis=1), carried)
        return (carried, produced)
    _, results = lax.scan(advance, jnp.zeros((H, HD, HD), jnp.float32), (query_blocks, key_blocks, value_blocks, block_logs))
    first_out = normalize(results.reshape(TOKEN_COUNT, H, HD), norm_gain)
    sparse_queries = sparse_query.reshape(QB, BLK, H, HD)
    sparse_keys = sparse_key.reshape(QB, BLK, H, HD)
    value_rows = first_out.reshape(QB, BLK, H, HD)
    offsets = jnp.arange(BLK, dtype=jnp.int32)
    scale = 1.0 / math.sqrt(HD)

    def attend(inputs):
        queries_here, chosen, block_index = inputs
        picked = jnp.maximum(chosen, 0).astype(jnp.int32)
        keys_here = sparse_keys[picked].reshape(NSEL * BLK, H, HD)
        values_here = value_rows[picked].reshape(NSEL * BLK, H, HD)
        scores = jnp.einsum('ihd,jhd->hij', queries_here.astype(jnp.float32), keys_here.astype(jnp.float32), precision=precise_mode) * scale
        key_pos = (chosen[:, None] * BLK + offsets[None, :]).reshape(-1)
        is_live = jnp.repeat(chosen >= 0, BLK)
        query_pos = block_index * BLK + offsets
        allowed = (is_live[None, :] & (key_pos[None, :] <= query_pos[:, None]))[None]
        scores = jnp.where(allowed, scores, -1e+30)
        row_max = lax.optimization_barrier(jnp.max(scores, axis=-1, keepdims=True))
        probs = jnp.where(allowed, jnp.exp(scores - row_max), 0.0)
        weights = (probs / lax.optimization_barrier(jnp.sum(probs, axis=-1, keepdims=True))).astype(jnp.bfloat16)
        return jnp.einsum('hij,jhd->ihd', weights.astype(jnp.float32), values_here.astype(jnp.float32), precision=precise_mode)
    second_out = lax.map(attend, (sparse_queries, block_pattern, jnp.arange(QB, dtype=jnp.int32))).reshape(TOKEN_COUNT, H, HD)
    layer_out = (first_out.astype(jnp.float32) + second_out).astype(jnp.bfloat16)
    return layer_out.reshape(TOKEN_COUNT, D)
```

```python
import functools
import math

import jax
import jax.numpy as jnp
from jax import lax
from jax.experimental import pallas as pl
from jax.experimental.pallas import tpu as pltpu
from jax.sharding import Mesh
from jax.sharding import PartitionSpec as P

BLK = 64
F32 = jnp.float32
BF16 = jnp.bfloat16
HIGHEST = lax.Precision.HIGHEST
VMEM = pl.BlockSpec(memory_space=pltpu.VMEM)
SMEM = pl.BlockSpec(memory_space=pltpu.SMEM)


def halves(x):
    high = x.astype(BF16)
    return high, (x - high.astype(F32)).astype(BF16)


def dot(a, b, dims):
    return lax.dot_general(a, b, (dims, ((), ())), preferred_element_type=F32)


def summed_logs(decay_ref):
    logs = jnp.log(decay_ref[...])
    length = logs.shape[1]
    row = lax.broadcasted_iota(jnp.int32, (length, length), 0)
    col = lax.broadcasted_iota(jnp.int32, (length, length), 1)
    upper = (row <= col).astype(F32)
    lower = (row >= col).astype(F32)
    along = lax.dot_general(logs, upper, (((1,), (0,)), ((), ())), precision=HIGHEST, preferred_element_type=F32)
    down = lax.dot_general(lower, logs, (((1,), (1,)), ((), ())), precision=HIGHEST, preferred_element_type=F32)
    return along, down, row >= col


def state_kernel(kv_ref, decay_ref, sent_ref, entering_ref):
    heads, chunks, width, _ = entering_ref.shape
    length = kv_ref.shape[1] // 2
    along, down, _ = summed_logs(decay_ref)
    for h in range(heads):
        columns = slice(h * width, (h + 1) * width)
        state = jnp.zeros((width, width), F32)
        whole = jnp.zeros((1, 1), F32)
        for c in range(chunks):
            at = h * chunks + c
            entering_ref[h, c] = state
            total = along[at : at + 1, length - 1 : length]
            keys = kv_ref[c, :length, columns].astype(F32)
            values = kv_ref[c, length:, columns]
            high, low = halves(keys * jnp.exp(total - down[:, at : at + 1]))
            state = jnp.exp(total) * state + dot(
                jnp.concatenate([high, low], 0), jnp.concatenate([values, values], 0), ((0,), (0,))
            )
            whole = whole + total
        sent_ref[h, :width, :] = state.astype(BF16)
        factor = jnp.exp(whole)
        first = factor.astype(BF16).astype(F32)
        second = (factor - first).astype(BF16).astype(F32)
        third = factor - first - second
        place = lax.broadcasted_iota(jnp.int32, (16, width), 0)
        sent_ref[h, width:, :] = jnp.where(
            place == 0, first, jnp.where(place == 1, second, jnp.where(place == 2, third, 0.0))
        ).astype(BF16)


def first_kernel(q_ref, kv_ref, decay_ref, entering_ref, gain_ref, *refs):
    earlier, out_ref = refs[:-1], refs[-1]
    heads, chunks, width, _ = entering_ref.shape
    length = q_ref.shape[1]
    along, down, causal = summed_logs(decay_ref)
    for h in range(heads):
        columns = slice(h * width, (h + 1) * width)
        carried = jnp.zeros((width, width), F32)
        factor = jnp.ones((1, 1), F32)
        for ref in earlier:
            carried = carried + factor * ref[h, :width, :].astype(F32)
            parts = ref[h, width:, :].astype(F32)
            factor = factor * (parts[0:1, 0:1] + parts[1:2, 0:1] + parts[2:3, 0:1])
        gain = gain_ref[h : h + 1, :]
        before = jnp.zeros((1, 1), F32)
        for c in range(chunks):
            at = h * chunks + c
            queries = q_ref[c, :, columns]
            keys = kv_ref[c, :length, columns]
            values = kv_ref[c, length:, columns]
            high, low = halves(entering_ref[h, c] + jnp.exp(before) * carried)
            outside = dot(
                jnp.concatenate([queries, queries], 1), jnp.concatenate([high, low], 0), ((1,), (0,))
            )
            down_here = down[:, at : at + 1]
            gap = jnp.where(causal, down_here - along[at : at + 1, :], 0.0)
            weights = jnp.where(causal, jnp.exp(gap), 0.0) * dot(queries, keys, ((1,), (1,)))
            inside = dot(
                jnp.concatenate(halves(weights), 1), jnp.concatenate([values, values], 0), ((1,), (0,))
            )
            raw = inside + jnp.exp(down_here) * outside
            scale = lax.rsqrt(jnp.mean(raw * raw, axis=-1, keepdims=True) + 1e-06)
            out_ref[c, :, columns] = (raw * scale * gain).astype(BF16)
            before = before + along[at : at + 1, length - 1 : length]


def weights_kernel(window_ref, q_ref, own_ref, earlier_ref, bias_ref, out_ref, keys_ref, picked_ref):
    tokens, width = q_ref.shape
    blocks = tokens // BLK
    picks = picked_ref.shape[0] // BLK
    keys_ref[:tokens, :] = earlier_ref[...]
    keys_ref[tokens:, :] = own_ref[...]
    row = lax.broadcasted_iota(jnp.int32, (BLK, picks * BLK), 0)
    col = lax.broadcasted_iota(jnp.int32, (BLK, picks * BLK), 1)
    causal = jnp.where((col >= BLK) | (col <= row), 0.0, -1e30)
    scale = 1.0 / math.sqrt(width)

    def one(b, _):
        for j in range(picks):
            start = pl.multiple_of(window_ref[b, j] * BLK, BLK)
            picked_ref[j * BLK : (j + 1) * BLK, :] = keys_ref[pl.ds(start, BLK), :]
        rows = pl.ds(pl.multiple_of(b * BLK, BLK), BLK)
        scores = dot(q_ref[rows, :], picked_ref[...], ((1,), (1,))) * scale
        scores = scores + (causal + bias_ref[pl.ds(b, 1), :])
        probs = jnp.exp(scores - jnp.max(scores, axis=-1, keepdims=True))
        out_ref[0, rows, :] = (probs / jnp.sum(probs, axis=-1, keepdims=True)).astype(BF16)
        return 0

    lax.fori_loop(0, blocks, one, 0)


def sum_kernel(window_ref, weights_ref, own_ref, earlier_ref, out_ref, values_ref, picked_ref):
    tokens, width = own_ref.shape
    blocks = tokens // BLK
    picks = picked_ref.shape[0] // BLK
    values_ref[:tokens, :] = earlier_ref[...]
    values_ref[tokens:, :] = own_ref[...]

    def one(b, _):
        for j in range(picks):
            start = pl.multiple_of(window_ref[b, j] * BLK, BLK)
            picked_ref[j * BLK : (j + 1) * BLK, :] = values_ref[pl.ds(start, BLK), :]
        rows = pl.ds(pl.multiple_of(b * BLK, BLK), BLK)
        second = dot(weights_ref[0, rows, :], picked_ref[...], ((1,), (0,)))
        out_ref[rows, :] = (own_ref[rows, :].astype(F32) + second).astype(BF16)
        return 0

    lax.fori_loop(0, blocks, one, 0)


PARAMS = pltpu.CompilerParams(vmem_limit_bytes=48 * 2**20)


def local(lin_query, lin_key, lin_value, sparse_query, sparse_key, decay, norm_gain, block_pattern):
    groups, inner = lax.axis_size("group"), lax.axis_size("inner")
    place, side = lax.axis_index("group"), lax.axis_index("side")
    ways = 2 * inner
    length, model = lin_query.shape
    width = norm_gain.shape[1]
    heads = norm_gain.shape[0] // 2
    here = heads * width
    tokens = ways * length
    blocks = tokens // BLK
    picks = block_pattern.shape[1]

    def pieces(x):
        return x.reshape(length, inner, 2, here).transpose(2, 1, 0, 3).reshape(ways, length, here)

    def exchange(x):
        return lax.all_to_all(x, ("side", "inner"), split_axis=0, concat_axis=0, tiled=True)

    def onward(x, steps=1):
        return lax.ppermute(x, "group", [(i, i + steps) for i in range(groups - steps)])

    span = decay.shape[1]
    flat = block_pattern.reshape(1, -1).astype(F32)
    flat = jnp.pad(flat, ((0, 0), (0, span - flat.shape[1])))
    mine = lax.dynamic_slice_in_dim(decay, side * heads, heads, 0)
    theirs = lax.dynamic_slice_in_dim(decay, (1 - side) * heads, heads, 0)
    other = lax.ppermute(jnp.concatenate([theirs, flat], 0), "side", [(0, 1), (1, 0)])
    own = jnp.concatenate([mine, flat], 0)
    both = jnp.where(side == 0, jnp.stack([own, other], 1), jnp.stack([other, own], 1))
    decays = both[:heads].reshape(heads * ways, length)
    pattern = both[heads, :, : block_pattern.size].reshape(blocks, picks).astype(jnp.int32)
    window = jnp.maximum(pattern - (place - 1) * blocks, 0)
    window = jnp.where(pattern >= 0, window, 0)
    bias = jnp.repeat(jnp.where(pattern >= 0, 0.0, -1e30).astype(F32), BLK, axis=1)
    gain = lax.dynamic_slice_in_dim(norm_gain, side * heads, heads, 0)

    sparse_keys = exchange(pieces(sparse_key))
    earlier_keys = onward(sparse_keys)
    keys_values = exchange(jnp.concatenate([pieces(lin_key), pieces(lin_value)], 1))
    queries = exchange(pieces(lin_query))
    sparse_queries = exchange(pieces(sparse_query))

    sent, entering = pl.pallas_call(
        state_kernel,
        out_shape=(
            jax.ShapeDtypeStruct((heads, width + 16, width), BF16),
            jax.ShapeDtypeStruct((heads, ways, width, width), F32),
        ),
        in_specs=[VMEM] * 2,
        out_specs=(VMEM, VMEM),
        compiler_params=PARAMS,
        name="state",
    )(keys_values, decays)
    states = [onward(sent, steps) for steps in range(1, groups)]
    first = pl.pallas_call(
        first_kernel,
        out_shape=jax.ShapeDtypeStruct((ways, length, here), BF16),
        in_specs=[VMEM] * (5 + len(states)),
        out_specs=VMEM,
        compiler_params=PARAMS,
        name="first",
    )(queries, keys_values, decays, entering, gain, *states)
    earlier_first = onward(first)

    column = pl.BlockSpec((tokens, width), lambda h: (0, h))
    table = pl.BlockSpec((1, tokens, picks * BLK), lambda h: (h, 0, 0))
    weights = pl.pallas_call(
        weights_kernel,
        out_shape=jax.ShapeDtypeStruct((heads, tokens, picks * BLK), BF16),
        grid=(heads,),
        in_specs=[SMEM, column, column, column, pl.BlockSpec((blocks, picks * BLK), lambda h: (0, 0))],
        out_specs=table,
        scratch_shapes=[pltpu.VMEM((2 * tokens, width), BF16), pltpu.VMEM((picks * BLK, width), BF16)],
        compiler_params=PARAMS,
        name="weights",
    )(
        window,
        sparse_queries.reshape(tokens, here),
        sparse_keys.reshape(tokens, here),
        earlier_keys.reshape(tokens, here),
        bias,
    )
    layer = pl.pallas_call(
        sum_kernel,
        out_shape=jax.ShapeDtypeStruct((tokens, here), BF16),
        grid=(heads,),
        in_specs=[SMEM, table, column, column],
        out_specs=column,
        scratch_shapes=[pltpu.VMEM((2 * tokens, width), BF16), pltpu.VMEM((picks * BLK, width), BF16)],
        compiler_params=PARAMS,
        name="sum",
    )(window, weights, first.reshape(tokens, here), earlier_first.reshape(tokens, here))
    back = exchange(layer.reshape(ways, length, here))
    return back.reshape(2, inner, length, here).transpose(2, 1, 0, 3).reshape(length, model)


def solution(mesh):
    spans, inner = mesh.devices.shape
    finer = Mesh(mesh.devices.reshape(spans // 2, 2, inner), ("group", "side", "inner"))
    rows = P(("group", "side", "inner"), None)
    placed = (rows,) * 5 + (P("inner", ("group", "side")), P("inner", None), P(("group", "side"), None))
    return jax.shard_map(local, mesh=finer, in_specs=placed, out_specs=rows, check_vma=False)
```

```python
import math

import jax
import jax.numpy as jnp
from jax import lax
from jax.experimental import pallas as pl
from jax.experimental.pallas import tpu as pltpu
from jax.sharding import Mesh
from jax.sharding import PartitionSpec as P

BLK = 64
STEP = 2
F32 = jnp.float32
BF16 = jnp.bfloat16
HIGHEST = lax.Precision.HIGHEST
VMEM = pl.BlockSpec(memory_space=pltpu.VMEM)
SMEM = pl.BlockSpec(memory_space=pltpu.SMEM)
ANY = pl.BlockSpec(memory_space=pl.ANY)
HBM = pl.BlockSpec(memory_space=pltpu.HBM)
PARAMS = pltpu.CompilerParams(vmem_limit_bytes=16 * 2**20)


def halves(x):
    high = x.astype(BF16)
    return high, (x - high.astype(F32)).astype(BF16)


def dot(a, b, dims):
    return lax.dot_general(a, b, (dims, ((), ())), preferred_element_type=F32)


def exact(a, b, dims):
    return lax.dot_general(a, b, (dims, ((), ())), precision=HIGHEST, preferred_element_type=F32)


def grid_of(shape):
    return lax.broadcasted_iota(jnp.int32, shape, 0), lax.broadcasted_iota(jnp.int32, shape, 1)


def summed_down(logs):
    length = logs.shape[1]
    row, col = grid_of((length, length))
    return exact((row >= col).astype(F32), logs, ((1,), (1,)))


def other_chunks(totals, chunks, later):
    count = totals.shape[1]
    row, col = grid_of((count, count))
    same = row // chunks == col // chunks
    taken = same & ((row > col) if later else (row < col))
    return exact(totals, taken.astype(F32), ((1,), (0,)))


def run_all(copies):
    for copy in copies:
        copy.start()
    for copy in copies:
        copy.wait()


def pieces_kernel(in_ref, *refs):
    out_ref, sem = refs[-2:]
    ways, _, here = out_ref.shape
    run_all([
        pltpu.make_async_copy(
            in_ref.at[:, pl.ds((d % (ways // 2) * 2 + d // (ways // 2)) * here, here)], out_ref.at[d], sem.at[d]
        )
        for d in range(ways)
    ])


def outward_kernel(columns_ref, *refs):
    ins, out_ref, sem = refs[:-2], refs[-2], refs[-1]
    length, here = ins[0].shape[0], out_ref.shape[2]
    run_all([
        pltpu.make_async_copy(
            ref.at[:, pl.ds(pl.multiple_of(columns_ref[k, 1], 128), here)],
            out_ref.at[k, pl.ds(n * length, length), :],
            sem.at[k, n],
        )
        for k in range(out_ref.shape[0])
        for n, ref in enumerate(ins)
    ])


def thirds(x):
    first = x.astype(BF16).astype(F32)
    second = (x - first).astype(BF16).astype(F32)
    return first, second, x - first - second


def parcel_kernel(count, extra, columns_ref, place_ref, *refs):
    ins, got_ref, table_ref = refs[:count], refs[count], refs[count + 1]
    scratch = 2 if extra else 1
    chips = got_ref.shape[0]
    outs, sem = refs[-scratch - chips : -scratch], refs[-1]
    length, here = ins[0].shape[0], got_ref.shape[2]
    core = place_ref[1]
    copies = []
    for k, out_ref in enumerate(outs):
        start = pl.multiple_of(columns_ref[k, 0], 128)
        for n, ref in enumerate(ins):
            copies.append(
                pltpu.make_async_copy(
                    ref.at[:, pl.ds(start, here)], out_ref.at[core, pl.ds(n * length, length), :], sem.at[k, n]
                )
            )
        copies.append(
            pltpu.make_async_copy(
                got_ref.at[k], out_ref.at[1 - core, pl.ds(0, count * length), :], sem.at[k, count]
            )
        )
    if extra:
        rows_ref = refs[-2]
        parts = jnp.concatenate(thirds(table_ref[...]), 0)
        if extra > parts.shape[0]:
            parts = jnp.concatenate([parts, jnp.zeros((extra - parts.shape[0], here), F32)], 0)
        for n in range(2):
            rows_ref[n] = parts.astype(BF16)
        copies.append(
            pltpu.make_async_copy(
                rows_ref, outs[chips // 2].at[:, pl.ds(count * length, extra), :], sem.at[0, count + 1]
            )
        )
    run_all(copies)


def gather_chunks(place_ref, refs, out_ref):
    for k, ref in enumerate(refs):
        chip = jnp.bitwise_xor(place_ref[0], k)
        out_ref[pl.ds(pl.multiple_of(2 * chip, 2), 2)] = ref[:, : out_ref.shape[1], :]


def state_kernel(place_ref, table_ref, *refs):
    parts, (sent_ref, start_ref, decay_ref, other_ref, kv_ref) = refs[:-5], refs[-5:]
    heads, width = sent_ref.shape[0], sent_ref.shape[2]
    chunks = kv_ref.shape[0]
    length = kv_ref.shape[1] // 2
    gather_chunks(place_ref, parts, kv_ref)
    size, here = table_ref.shape
    got = parts[len(parts) // 2][0, 2 * length :, :].astype(F32)
    mine, theirs = table_ref[...], got[:size] + got[size : 2 * size] + got[2 * size : 3 * size]
    leads = place_ref[2] == 0
    spans = (jnp.where(leads, mine, theirs), jnp.where(leads, theirs, mine))
    span = size * here // (heads + 1)
    for n, table in enumerate(spans):
        for h in range(heads):
            for t in range(chunks // 2):
                row, lane = divmod(h * span + t * length, here)
                at = h * chunks + n * (chunks // 2) + t
                decay_ref[at : at + 1, :] = table[row : row + 1, lane : lane + length]
        other_ref[n] = table[size - span // here :, :]
    down = summed_down(jnp.log(decay_ref[...]))
    totals = down[length - 1 : length, :]
    left = jnp.exp(totals - down)
    kept = jnp.exp(totals)
    factors = jnp.exp(totals + other_chunks(totals, chunks, True))
    place = lax.broadcasted_iota(jnp.int32, (16, width), 0)
    for h in range(heads):
        columns = slice(h * width, (h + 1) * width)
        state = jnp.zeros((width, width), F32)
        for c in range(chunks):
            at = h * chunks + c
            if c:
                high, low = halves(state)
                start_ref[h, c, :width, :] = high
                start_ref[h, c, width:, :] = low
            keys = kv_ref[c, :length, columns].astype(F32)
            values = kv_ref[c, length:, columns]
            high, low = halves(keys * left[:, at : at + 1])
            state = kept[:, at : at + 1] * state + dot(
                jnp.concatenate([high, low], 0), jnp.concatenate([values, values], 0), ((0,), (0,))
            )
        sent_ref[h, :width, :] = state.astype(BF16)
        factor = factors[:, h * chunks : h * chunks + 1]
        first, second, third = thirds(factor)
        sent_ref[h, width:, :] = jnp.where(
            place == 0, first, jnp.where(place == 1, second, jnp.where(place == 2, third, 0.0))
        ).astype(BF16)


def inside_kernel(count, place_ref, decay_ref, start_ref, *refs):
    q_parts, kv_parts, (raw_ref, q_ref, kv_ref) = refs[:count], refs[count : 2 * count], refs[2 * count :]
    chunks, length, here = q_ref.shape
    heads = decay_ref.shape[0] // chunks
    width = here // heads
    gather_chunks(place_ref, q_parts, q_ref)
    gather_chunks(place_ref, kv_parts, kv_ref)
    logs = jnp.log(decay_ref[...])
    row, col = grid_of((length, length))
    along = exact(logs, (row <= col).astype(F32), ((1,), (0,)))
    down = summed_down(logs)
    lifts = jnp.exp(down)
    causal = row >= col
    for h in range(heads):
        columns = slice(h * width, (h + 1) * width)
        for c in range(chunks):
            at = h * chunks + c
            queries = q_ref[c, :, columns]
            keys = kv_ref[c, :length, columns]
            values = kv_ref[c, length:, columns]
            gap = jnp.where(causal, down[:, at : at + 1] - along[at : at + 1, :], 0.0)
            weights = jnp.where(causal, jnp.exp(gap), 0.0) * dot(queries, keys, ((1,), (1,)))
            raw = dot(jnp.concatenate(halves(weights), 1), jnp.concatenate([values, values], 0), ((1,), (0,)))
            if c:
                raw = raw + lifts[:, at : at + 1] * dot(
                    jnp.concatenate([queries, queries], 1), start_ref[h, c], ((1,), (0,))
                )
            raw_ref[c, :, columns] = raw


def first_kernel(raw_ref, q_ref, decay_ref, gain_ref, *refs):
    earlier, out_ref = refs[:-2], refs[-1]
    chunks, length, here = q_ref.shape
    heads, width = gain_ref.shape
    down = summed_down(jnp.log(decay_ref[...]))
    lifts = jnp.exp(down + other_chunks(down[length - 1 : length, :], chunks, False))
    for h in range(heads):
        columns = slice(h * width, (h + 1) * width)
        carried = jnp.zeros((width, width), F32)
        factor = jnp.ones((1, 1), F32)
        for ref in earlier:
            carried = carried + factor * ref[h, :width, :].astype(F32)
            parts = ref[h, width:, :].astype(F32)
            factor = factor * (parts[0:1, 0:1] + parts[1:2, 0:1] + parts[2:3, 0:1])
        both = jnp.concatenate(halves(carried), 0)
        gain = gain_ref[h : h + 1, :]
        for c in range(chunks):
            at = h * chunks + c
            queries = q_ref[c, :, columns]
            outside = dot(jnp.concatenate([queries, queries], 1), both, ((1,), (0,)))
            raw = raw_ref[c, :, columns] + lifts[:, at : at + 1] * outside
            scale = lax.rsqrt(jnp.mean(raw * raw, axis=-1, keepdims=True) + 1e-06)
            out_ref[c, :, columns] = (raw * scale * gain).astype(BF16)


def pick(window_ref, b, source_ref, picked_ref):
    for j in range(picked_ref.shape[0] // BLK):
        start = pl.multiple_of(window_ref[b, j] * BLK, BLK)
        picked_ref[j * BLK : (j + 1) * BLK, :] = source_ref[pl.ds(start, BLK), :]


def weights_kernel(window_ref, own_ref, earlier_ref, bias_ref, q_ref, out_ref, keys_ref, picked_ref):
    tokens, here = own_ref.shape
    heads = out_ref.shape[0]
    width = here // heads
    picks = picked_ref.shape[1] // BLK
    group = pl.program_id(0)

    @pl.when(group == 0)
    def _():
        keys_ref[:tokens, :] = earlier_ref[...]
        keys_ref[tokens:, :] = own_ref[...]

    row, col = grid_of((BLK, picks * BLK))
    causal = jnp.where((col >= BLK) | (col <= row), 0.0, -1e30)
    scale = 1.0 / math.sqrt(width)
    for t in range(STEP):
        b = group * STEP + t
        pick(window_ref, b, keys_ref, picked_ref.at[t])
        bias = causal + bias_ref[pl.ds(b, 1), :]
        for h in range(heads):
            columns = slice(h * width, (h + 1) * width)
            scores = dot(q_ref[t * BLK : (t + 1) * BLK, columns], picked_ref[t, :, columns], ((1,), (1,))) * scale
            scores = scores + bias
            probs = jnp.exp(scores - jnp.max(scores, axis=-1, keepdims=True))
            share = 1.0 / jnp.sum(probs, axis=-1, keepdims=True)
            out_ref[h, t * BLK : (t + 1) * BLK, :] = (probs * share).astype(BF16)


def sum_kernel(window_ref, weights_ref, own_ref, earlier_ref, out_ref, values_ref, picked_ref):
    tokens, here = own_ref.shape
    heads = weights_ref.shape[0]
    width = here // heads
    group = pl.program_id(0)

    @pl.when(group == 0)
    def _():
        values_ref[:tokens, :] = earlier_ref[...]
        values_ref[tokens:, :] = own_ref[...]

    for t in range(STEP):
        b = group * STEP + t
        pick(window_ref, b, values_ref, picked_ref.at[t])
        rows = pl.ds(pl.multiple_of(b * BLK, BLK), BLK)
        for h in range(heads):
            columns = slice(h * width, (h + 1) * width)
            second = dot(weights_ref[h, t * BLK : (t + 1) * BLK, :], picked_ref[t, :, columns], ((1,), (0,)))
            out_ref[t * BLK : (t + 1) * BLK, columns] = (own_ref[rows, columns].astype(F32) + second).astype(BF16)


def local(lin_query, lin_key, lin_value, sparse_query, sparse_key, decay, norm_gain, block_pattern):
    groups, inner = lax.axis_size("group"), lax.axis_size("inner")
    level, side, index = lax.axis_index("group"), lax.axis_index("side"), lax.axis_index("inner")
    ways = 2 * inner
    chips = ways // 2
    length, model = lin_query.shape
    width = norm_gain.shape[1]
    heads = norm_gain.shape[0] // 2
    here = heads * width
    tokens = ways * length
    blocks = tokens // BLK
    picks = block_pattern.shape[1]

    chip, core = side * (inner // 2) + index // 2, index % 2
    place = jnp.stack([chip, core, side]).astype(jnp.int32)
    peers = jnp.bitwise_xor(chip, jnp.arange(chips, dtype=jnp.int32))
    cores = jnp.stack([core, 1 - core])
    indices = (peers % (inner // 2))[:, None] * 2 + cores[None, :]
    columns = ((indices * 2 + (peers // (inner // 2))[:, None]) * here).astype(jnp.int32)

    def swap(x):
        return lax.ppermute(x, ("side", "inner"), [(i, i ^ 1) for i in range(ways)])

    def spread(*arrays, table=None, after=()):
        rows = len(arrays) * length
        extra = 0 if table is None else -(-3 * table.shape[0] // 16) * 16
        after = after if table is None else (table, *after)
        out = pl.pallas_call(
            outward_kernel,
            out_shape=pltpu.HBM((chips, rows, here), BF16),
            in_specs=[SMEM] + [VMEM] * len(arrays),
            out_specs=HBM,
            scratch_shapes=[pltpu.SemaphoreType.DMA((chips, len(arrays)))],
            compiler_params=PARAMS,
            name="outward",
        )(columns, *arrays)
        parcels = pl.pallas_call(
            lambda *refs: parcel_kernel(len(arrays), extra, *refs),
            out_shape=[
                pltpu.HBM((2, rows + (extra if k == chips // 2 else 0), here), BF16) for k in range(chips)
            ],
            in_specs=[SMEM, SMEM] + [VMEM] * (len(arrays) + 1) + [VMEM] * bool(extra) + [ANY] * (len(after) - bool(extra)),
            out_specs=[HBM] * chips,
            scratch_shapes=[pltpu.VMEM((2, extra, here), BF16)] * bool(extra)
            + [pltpu.SemaphoreType.DMA((chips, len(arrays) + 2))],
            compiler_params=PARAMS,
            name="parcels",
        )(columns, place, *arrays, swap(out), *after)
        return parcels, [parcels[0]] + [
            lax.ppermute(x, ("side", "inner"), [(i, i ^ (2 * k)) for i in range(ways)])
            for k, x in enumerate(parcels)
            if k
        ]

    def exchange(x, after=()):
        pieces = pl.pallas_call(
            pieces_kernel,
            out_shape=pltpu.HBM((ways, length, here), BF16),
            in_specs=[VMEM] + [ANY] * len(after),
            out_specs=HBM,
            scratch_shapes=[pltpu.SemaphoreType.DMA((ways,))],
            compiler_params=PARAMS,
            name="pieces",
        )(x, *after)
        return lax.all_to_all(pieces, ("side", "inner"), split_axis=0, concat_axis=0, tiled=True)

    def onward(x, steps=1):
        return lax.ppermute(x, "group", [(i, i + steps) for i in range(groups - steps)])

    span = decay.shape[1]
    flat = block_pattern.reshape(1, -1).astype(F32)
    flat = jnp.pad(flat, ((0, 0), (0, span - flat.shape[1])))

    def table(first_head):
        return jnp.concatenate([lax.dynamic_slice_in_dim(decay, first_head, heads, 0), flat], 0).reshape(-1, here)

    mine = table(side * heads)
    gain = lax.dynamic_slice_in_dim(norm_gain, side * heads, heads, 0)

    sparse_keys = exchange(sparse_key)
    parcels, kv_parts = spread(lin_key, lin_value, table=table((1 - side) * heads))
    _, q_parts = spread(lin_query, after=kv_parts[1:3])
    earlier_keys = onward(sparse_keys)

    sent, starts, decays, others = pl.pallas_call(
        state_kernel,
        out_shape=(
            jax.ShapeDtypeStruct((heads, width + 16, width), BF16),
            jax.ShapeDtypeStruct((heads, ways, 2 * width, width), BF16),
            jax.ShapeDtypeStruct((heads * ways, length), F32),
            jax.ShapeDtypeStruct((2, span // here, here), F32),
        ),
        in_specs=[SMEM, VMEM] + [VMEM] * chips,
        out_specs=(VMEM,) * 4,
        scratch_shapes=[pltpu.VMEM((ways, 2 * length, here), BF16)],
        compiler_params=PARAMS,
        name="state",
    )(place, mine, *kv_parts)
    pattern = others.reshape(2, span)[:, : block_pattern.size].reshape(blocks, picks).astype(jnp.int32)
    window = jnp.where(pattern >= 0, pattern - (level - 1) * blocks, 0)
    bias = jnp.repeat(jnp.where(pattern >= 0, 0.0, -1e30).astype(F32), BLK, axis=1)
    states = [onward(sent, steps) for steps in range(1, groups)]
    raw, queries = pl.pallas_call(
        lambda *refs: inside_kernel(chips, *refs),
        out_shape=(
            jax.ShapeDtypeStruct((ways, length, here), F32),
            jax.ShapeDtypeStruct((ways, length, here), BF16),
        ),
        in_specs=[SMEM, VMEM, VMEM] + [VMEM] * (2 * chips),
        out_specs=(VMEM, VMEM),
        scratch_shapes=[pltpu.VMEM((ways, 2 * length, here), BF16)],
        compiler_params=PARAMS,
        cost_estimate=pl.CostEstimate(flops=2**31, bytes_accessed=6 * 2**20, transcendentals=2**19),
        name="inside",
    )(place, decays, starts, *q_parts, *kv_parts)
    sparse_queries = exchange(sparse_query, after=(raw,))
    first = pl.pallas_call(
        first_kernel,
        out_shape=jax.ShapeDtypeStruct((ways, length, here), BF16),
        in_specs=[VMEM] * (4 + len(states)) + [ANY],
        out_specs=VMEM,
        compiler_params=PARAMS,
        name="first",
    )(raw, queries, decays, gain, *states, earlier_keys)
    earlier_first = onward(first)

    steps = blocks // STEP
    rows = STEP * BLK
    whole = pl.BlockSpec((tokens, here), lambda g: (0, 0))
    part = pl.BlockSpec((rows, here), lambda g: (g, 0))
    table = pl.BlockSpec((heads, rows, picks * BLK), lambda g: (0, g, 0))
    weights = pl.pallas_call(
        weights_kernel,
        out_shape=jax.ShapeDtypeStruct((heads, tokens, picks * BLK), BF16),
        grid=(steps,),
        in_specs=[SMEM, whole, whole, pl.BlockSpec((blocks, picks * BLK), lambda g: (0, 0)), part],
        out_specs=table,
        scratch_shapes=[
            pltpu.VMEM((2 * tokens, here), BF16),
            pltpu.VMEM((STEP, picks * BLK, here), BF16),
        ],
        compiler_params=PARAMS,
        cost_estimate=pl.CostEstimate(flops=2**31, bytes_accessed=8 * 2**20, transcendentals=2**21),
        name="weights",
    )(
        window,
        sparse_keys.reshape(tokens, here),
        earlier_keys.reshape(tokens, here),
        bias,
        sparse_queries.reshape(tokens, here),
    )
    layer = pl.pallas_call(
        sum_kernel,
        out_shape=jax.ShapeDtypeStruct((tokens, here), BF16),
        grid=(steps,),
        in_specs=[SMEM, table, whole, whole],
        out_specs=part,
        scratch_shapes=[
            pltpu.VMEM((2 * tokens, here), BF16),
            pltpu.VMEM((STEP, picks * BLK, here), BF16),
        ],
        compiler_params=PARAMS,
        name="sum",
    )(window, weights, first.reshape(tokens, here), earlier_first.reshape(tokens, here))
    back = lax.all_to_all(
        layer.reshape(ways, length, here), ("side", "inner"), split_axis=0, concat_axis=0, tiled=True
    )
    return back.reshape(2, inner, length, here).transpose(2, 1, 0, 3).reshape(length, model)


def solution(mesh):
    spans, inner = mesh.devices.shape
    finer = Mesh(mesh.devices.reshape(spans // 2, 2, inner), ("group", "side", "inner"))
    rows = P(("group", "side", "inner"), None)
    placed = (rows,) * 5 + (P("inner", ("group", "side")), P("inner", None), P(("group", "side"), None))
    return jax.shard_map(local, mesh=finer, in_specs=placed, out_specs=rows, check_vma=False)
```

```python
import math

import jax
import jax.numpy as jnp
from jax import lax
from jax.experimental import pallas as pl
from jax.experimental.pallas import tpu as pltpu
from jax.sharding import Mesh
from jax.sharding import PartitionSpec as P

BLK = 64
STEP = 2
F32 = jnp.float32
BF16 = jnp.bfloat16
HIGHEST = lax.Precision.HIGHEST
VMEM = pl.BlockSpec(memory_space=pltpu.VMEM)
SMEM = pl.BlockSpec(memory_space=pltpu.SMEM)
ANY = pl.BlockSpec(memory_space=pl.ANY)
HBM = pl.BlockSpec(memory_space=pltpu.HBM)
PARAMS = pltpu.CompilerParams(vmem_limit_bytes=16 * 2**20)


def halves(x):
    high = x.astype(BF16)
    return high, (x - high.astype(F32)).astype(BF16)


def dot(a, b, dims):
    return lax.dot_general(a, b, (dims, ((), ())), preferred_element_type=F32)


def exact(a, b, dims):
    return lax.dot_general(a, b, (dims, ((), ())), precision=HIGHEST, preferred_element_type=F32)


def grid_of(shape):
    return lax.broadcasted_iota(jnp.int32, shape, 0), lax.broadcasted_iota(jnp.int32, shape, 1)


def summed_down(logs):
    length = logs.shape[1]
    row, col = grid_of((length, length))
    return exact((row >= col).astype(F32), logs, ((1,), (1,)))


def other_chunks(totals, chunks, later):
    count = totals.shape[1]
    row, col = grid_of((count, count))
    same = row // chunks == col // chunks
    taken = same & ((row > col) if later else (row < col))
    return exact(totals, taken.astype(F32), ((1,), (0,)))


def run_all(copies):
    for copy in copies:
        copy.start()
    for copy in copies:
        copy.wait()


def pieces_kernel(in_ref, *refs):
    out_ref, sem = refs[-2:]
    ways, _, here = out_ref.shape
    run_all([
        pltpu.make_async_copy(
            in_ref.at[:, pl.ds((d % (ways // 2) * 2 + d // (ways // 2)) * here, here)], out_ref.at[d], sem.at[d]
        )
        for d in range(ways)
    ])


def outward_kernel(columns_ref, *refs):
    ins, out_ref, sem = refs[:-2], refs[-2], refs[-1]
    length, here = ins[0].shape[0], out_ref.shape[2]
    run_all([
        pltpu.make_async_copy(
            ref.at[:, pl.ds(pl.multiple_of(columns_ref[k, 1], 128), here)],
            out_ref.at[k, pl.ds(n * length, length), :],
            sem.at[k, n],
        )
        for k in range(out_ref.shape[0])
        for n, ref in enumerate(ins)
    ])


def thirds(x):
    first = x.astype(BF16).astype(F32)
    second = (x - first).astype(BF16).astype(F32)
    return first, second, x - first - second


def parcel_kernel(count, extra, columns_ref, place_ref, *refs):
    ins, got_ref, table_ref = refs[:count], refs[count], refs[count + 1]
    scratch = 2 if extra else 1
    chips = got_ref.shape[0]
    outs, sem = refs[-scratch - chips : -scratch], refs[-1]
    length, here = ins[0].shape[0], got_ref.shape[2]
    core = place_ref[1]
    copies = []
    for k, out_ref in enumerate(outs):
        start = pl.multiple_of(columns_ref[k, 0], 128)
        for n, ref in enumerate(ins):
            copies.append(
                pltpu.make_async_copy(
                    ref.at[:, pl.ds(start, here)], out_ref.at[core, pl.ds(n * length, length), :], sem.at[k, n]
                )
            )
        copies.append(
            pltpu.make_async_copy(
                got_ref.at[k], out_ref.at[1 - core, pl.ds(0, count * length), :], sem.at[k, count]
            )
        )
    if extra:
        rows_ref = refs[-2]
        parts = jnp.concatenate(thirds(table_ref[...]), 0)
        if extra > parts.shape[0]:
            parts = jnp.concatenate([parts, jnp.zeros((extra - parts.shape[0], here), F32)], 0)
        for n in range(2):
            rows_ref[n] = parts.astype(BF16)
        copies.append(
            pltpu.make_async_copy(
                rows_ref, outs[chips // 2].at[:, pl.ds(count * length, extra), :], sem.at[0, count + 1]
            )
        )
    run_all(copies)


def gather_chunks(place_ref, refs, out_ref):
    for k, ref in enumerate(refs):
        chip = jnp.bitwise_xor(place_ref[0], k)
        out_ref[pl.ds(pl.multiple_of(2 * chip, 2), 2)] = ref[:, : out_ref.shape[1], :]


def state_kernel(place_ref, table_ref, *refs):
    parts, (sent_ref, start_ref, decay_ref, other_ref, kv_ref) = refs[:-5], refs[-5:]
    heads, width = sent_ref.shape[0], sent_ref.shape[2]
    chunks = kv_ref.shape[0]
    length = kv_ref.shape[1] // 2
    gather_chunks(place_ref, parts, kv_ref)
    size, here = table_ref.shape
    got = parts[len(parts) // 2][0, 2 * length :, :].astype(F32)
    mine, theirs = table_ref[...], got[:size] + got[size : 2 * size] + got[2 * size : 3 * size]
    leads = place_ref[2] == 0
    spans = (jnp.where(leads, mine, theirs), jnp.where(leads, theirs, mine))
    span = size * here // (heads + 1)
    for n, table in enumerate(spans):
        for h in range(heads):
            for t in range(chunks // 2):
                row, lane = divmod(h * span + t * length, here)
                at = h * chunks + n * (chunks // 2) + t
                decay_ref[at : at + 1, :] = table[row : row + 1, lane : lane + length]
        other_ref[n] = table[size - span // here :, :]
    down = summed_down(jnp.log(decay_ref[...]))
    totals = down[length - 1 : length, :]
    left = jnp.exp(totals - down)
    kept = jnp.exp(totals)
    factors = jnp.exp(totals + other_chunks(totals, chunks, True))
    place = lax.broadcasted_iota(jnp.int32, (16, width), 0)
    for h in range(heads):
        columns = slice(h * width, (h + 1) * width)
        state = jnp.zeros((width, width), F32)
        for c in range(chunks):
            at = h * chunks + c
            if c:
                high, low = halves(state)
                start_ref[h, c, :width, :] = high
                start_ref[h, c, width:, :] = low
            keys = kv_ref[c, :length, columns].astype(F32)
            values = kv_ref[c, length:, columns]
            high, low = halves(keys * left[:, at : at + 1])
            state = kept[:, at : at + 1] * state + dot(
                jnp.concatenate([high, low], 0), jnp.concatenate([values, values], 0), ((0,), (0,))
            )
        sent_ref[h, :width, :] = state.astype(BF16)
        factor = factors[:, h * chunks : h * chunks + 1]
        first, second, third = thirds(factor)
        sent_ref[h, width:, :] = jnp.where(
            place == 0, first, jnp.where(place == 1, second, jnp.where(place == 2, third, 0.0))
        ).astype(BF16)


def inside_kernel(count, place_ref, decay_ref, start_ref, *refs):
    q_parts, kv_parts, (raw_ref, q_ref, kv_ref) = refs[:count], refs[count : 2 * count], refs[2 * count :]
    chunks, length, here = q_ref.shape
    heads = decay_ref.shape[0] // chunks
    width = here // heads
    gather_chunks(place_ref, q_parts, q_ref)
    gather_chunks(place_ref, kv_parts, kv_ref)
    logs = jnp.log(decay_ref[...])
    row, col = grid_of((length, length))
    along = exact(logs, (row <= col).astype(F32), ((1,), (0,)))
    down = summed_down(logs)
    lifts = jnp.exp(down)
    causal = row >= col
    for h in range(heads):
        columns = slice(h * width, (h + 1) * width)
        for c in range(chunks):
            at = h * chunks + c
            queries = q_ref[c, :, columns]
            keys = kv_ref[c, :length, columns]
            values = kv_ref[c, length:, columns]
            gap = jnp.where(causal, down[:, at : at + 1] - along[at : at + 1, :], 0.0)
            weights = jnp.where(causal, jnp.exp(gap), 0.0) * dot(queries, keys, ((1,), (1,)))
            raw = dot(jnp.concatenate(halves(weights), 1), jnp.concatenate([values, values], 0), ((1,), (0,)))
            if c:
                raw = raw + lifts[:, at : at + 1] * dot(
                    jnp.concatenate([queries, queries], 1), start_ref[h, c], ((1,), (0,))
                )
            raw_ref[c, :, columns] = raw


def first_kernel(raw_ref, q_ref, decay_ref, gain_ref, *refs):
    earlier, outs = refs[:-3], refs[-2:]
    chunks, length, here = q_ref.shape
    heads, width = gain_ref.shape
    down = summed_down(jnp.log(decay_ref[...]))
    lifts = jnp.exp(down + other_chunks(down[length - 1 : length, :], chunks, False))
    for h in range(heads):
        columns = slice(h * width, (h + 1) * width)
        carried = jnp.zeros((width, width), F32)
        factor = jnp.ones((1, 1), F32)
        for ref in earlier:
            carried = carried + factor * ref[h, :width, :].astype(F32)
            parts = ref[h, width:, :].astype(F32)
            factor = factor * (parts[0:1, 0:1] + parts[1:2, 0:1] + parts[2:3, 0:1])
        both = jnp.concatenate(halves(carried), 0)
        gain = gain_ref[h : h + 1, :]
        place = h % (heads // 2)
        for c in range(chunks):
            at = h * chunks + c
            queries = q_ref[c, :, columns]
            outside = dot(jnp.concatenate([queries, queries], 1), both, ((1,), (0,)))
            raw = raw_ref[c, :, columns] + lifts[:, at : at + 1] * outside
            scale = lax.rsqrt(jnp.mean(raw * raw, axis=-1, keepdims=True) + 1e-06)
            outs[h // (heads // 2)][c, :, place * width : (place + 1) * width] = (raw * scale * gain).astype(BF16)


def pick(window_ref, b, source_ref, picked_ref):
    for j in range(picked_ref.shape[0] // BLK):
        start = pl.multiple_of(window_ref[b, j] * BLK, BLK)
        picked_ref[j * BLK : (j + 1) * BLK, :] = source_ref[pl.ds(start, BLK), :]


def weights_kernel(window_ref, own_ref, earlier_ref, bias_ref, q_ref, out_ref, keys_ref, picked_ref):
    tokens, here = own_ref.shape
    heads = out_ref.shape[0]
    width = here // heads
    picks = picked_ref.shape[1] // BLK
    group = pl.program_id(0)

    @pl.when(group == 0)
    def _():
        keys_ref[:tokens, :] = earlier_ref[...]
        keys_ref[tokens:, :] = own_ref[...]

    row, col = grid_of((BLK, picks * BLK))
    causal = jnp.where((col >= BLK) | (col <= row), 0.0, -1e30)
    scale = 1.0 / math.sqrt(width)
    for t in range(STEP):
        b = group * STEP + t
        pick(window_ref, b, keys_ref, picked_ref.at[t])
        bias = causal + bias_ref[pl.ds(b, 1), :]
        for h in range(heads):
            columns = slice(h * width, (h + 1) * width)
            scores = dot(q_ref[t * BLK : (t + 1) * BLK, columns], picked_ref[t, :, columns], ((1,), (1,))) * scale
            scores = scores + bias
            probs = jnp.exp(scores - jnp.max(scores, axis=-1, keepdims=True))
            share = 1.0 / jnp.sum(probs, axis=-1, keepdims=True)
            out_ref[h, t * BLK : (t + 1) * BLK, :] = (probs * share).astype(BF16)


def sum_kernel(order_ref, window_ref, weights_ref, own_ref, earlier_ref, *refs):
    outs, values_ref, picked_ref = refs[:-2], refs[-2], refs[-1]
    tokens, here = own_ref.shape
    heads, length, _ = weights_ref.shape
    width = here // heads
    step = pl.program_id(0)

    @pl.when(step == 0)
    def _():
        values_ref[:tokens, :] = earlier_ref[...]
        values_ref[tokens:, :] = own_ref[...]

    results = []
    for t in range(length // BLK):
        b = order_ref[step] * (length // BLK) + t
        pick(window_ref, b, values_ref, picked_ref.at[t])
        rows = pl.ds(pl.multiple_of(b * BLK, BLK), BLK)
        for h in range(heads):
            columns = slice(h * width, (h + 1) * width)
            second = dot(weights_ref[h, t * BLK : (t + 1) * BLK, :], picked_ref[t, :, columns], ((1,), (0,)))
            results.append((t, columns, (own_ref[rows, columns].astype(F32) + second).astype(BF16)))
    for k, out_ref in enumerate(outs):

        @pl.when(step // 2 == k)
        def _(out_ref=out_ref):
            for t, columns, result in results:
                out_ref[0, t * BLK : (t + 1) * BLK, columns] = result


def join_kernel(columns_ref, *refs):
    parts, out_ref = refs[:-1], refs[-1]
    here = parts[0].shape[2]
    chips = columns_ref.shape[0]
    for n, ref in enumerate(parts):
        half, k, core = n // (2 * chips), n // 2 % chips, n % 2
        start = pl.multiple_of(columns_ref[k, core] + half * here, 128)
        out_ref[:, pl.ds(start, here)] = ref[0]


def local(lin_query, lin_key, lin_value, sparse_query, sparse_key, decay, norm_gain, block_pattern):
    groups, inner = lax.axis_size("group"), lax.axis_size("inner")
    level, side, index = lax.axis_index("group"), lax.axis_index("side"), lax.axis_index("inner")
    ways = 2 * inner
    chips = ways // 2
    length, model = lin_query.shape
    width = norm_gain.shape[1]
    heads = norm_gain.shape[0] // 2
    here = heads * width
    tokens = ways * length
    blocks = tokens // BLK
    picks = block_pattern.shape[1]

    chip, core = side * (inner // 2) + index // 2, index % 2
    place = jnp.stack([chip, core, side]).astype(jnp.int32)
    peers = jnp.bitwise_xor(chip, jnp.arange(chips, dtype=jnp.int32))
    cores = jnp.stack([core, 1 - core])
    indices = (peers % (inner // 2))[:, None] * 2 + cores[None, :]
    columns = ((indices * 2 + (peers // (inner // 2))[:, None]) * here).astype(jnp.int32)

    def swap(x):
        return lax.ppermute(x, ("side", "inner"), [(i, i ^ 1) for i in range(ways)])

    def spread(*arrays, table=None, after=()):
        rows = len(arrays) * length
        extra = 0 if table is None else -(-3 * table.shape[0] // 16) * 16
        after = after if table is None else (table, *after)
        out = pl.pallas_call(
            outward_kernel,
            out_shape=pltpu.HBM((chips, rows, here), BF16),
            in_specs=[SMEM] + [VMEM] * len(arrays),
            out_specs=HBM,
            scratch_shapes=[pltpu.SemaphoreType.DMA((chips, len(arrays)))],
            compiler_params=PARAMS,
            name="outward",
        )(columns, *arrays)
        parcels = pl.pallas_call(
            lambda *refs: parcel_kernel(len(arrays), extra, *refs),
            out_shape=[
                pltpu.HBM((2, rows + (extra if k == chips // 2 else 0), here), BF16) for k in range(chips)
            ],
            in_specs=[SMEM, SMEM] + [VMEM] * (len(arrays) + 1) + [VMEM] * bool(extra) + [ANY] * (len(after) - bool(extra)),
            out_specs=[HBM] * chips,
            scratch_shapes=[pltpu.VMEM((2, extra, here), BF16)] * bool(extra)
            + [pltpu.SemaphoreType.DMA((chips, len(arrays) + 2))],
            compiler_params=PARAMS,
            name="parcels",
        )(columns, place, *arrays, swap(out), *after)
        return parcels, [parcels[0]] + [
            lax.ppermute(x, ("side", "inner"), [(i, i ^ (2 * k)) for i in range(ways)])
            for k, x in enumerate(parcels)
            if k
        ]

    def exchange(x, after=()):
        pieces = pl.pallas_call(
            pieces_kernel,
            out_shape=pltpu.HBM((ways, length, here), BF16),
            in_specs=[VMEM] + [ANY] * len(after),
            out_specs=HBM,
            scratch_shapes=[pltpu.SemaphoreType.DMA((ways,))],
            compiler_params=PARAMS,
            name="pieces",
        )(x, *after)
        return lax.all_to_all(pieces, ("side", "inner"), split_axis=0, concat_axis=0, tiled=True)

    def onward(x, steps=1):
        return lax.ppermute(x, "group", [(i, i + steps) for i in range(groups - steps)])

    span = decay.shape[1]
    flat = block_pattern.reshape(1, -1).astype(F32)
    flat = jnp.pad(flat, ((0, 0), (0, span - flat.shape[1])))

    def table(first_head):
        return jnp.concatenate([lax.dynamic_slice_in_dim(decay, first_head, heads, 0), flat], 0).reshape(-1, here)

    mine = table(side * heads)
    gain = lax.dynamic_slice_in_dim(norm_gain, side * heads, heads, 0)

    sparse_keys = exchange(sparse_key)
    parcels, kv_parts = spread(lin_key, lin_value, table=table((1 - side) * heads))
    _, q_parts = spread(lin_query, after=kv_parts[1:3])
    earlier_keys = onward(sparse_keys)

    sent, starts, decays, others = pl.pallas_call(
        state_kernel,
        out_shape=(
            jax.ShapeDtypeStruct((heads, width + 16, width), BF16),
            jax.ShapeDtypeStruct((heads, ways, 2 * width, width), BF16),
            jax.ShapeDtypeStruct((heads * ways, length), F32),
            jax.ShapeDtypeStruct((2, span // here, here), F32),
        ),
        in_specs=[SMEM, VMEM] + [VMEM] * chips,
        out_specs=(VMEM,) * 4,
        scratch_shapes=[pltpu.VMEM((ways, 2 * length, here), BF16)],
        compiler_params=PARAMS,
        name="state",
    )(place, mine, *kv_parts)
    pattern = others.reshape(2, span)[:, : block_pattern.size].reshape(blocks, picks).astype(jnp.int32)
    window = jnp.where(pattern >= 0, pattern - (level - 1) * blocks, 0)
    bias = jnp.repeat(jnp.where(pattern >= 0, 0.0, -1e30).astype(F32), BLK, axis=1)
    states = [onward(sent, steps) for steps in range(1, groups)]
    raw, queries = pl.pallas_call(
        lambda *refs: inside_kernel(chips, *refs),
        out_shape=(
            jax.ShapeDtypeStruct((ways, length, here), F32),
            jax.ShapeDtypeStruct((ways, length, here), BF16),
        ),
        in_specs=[SMEM, VMEM, VMEM] + [VMEM] * (2 * chips),
        out_specs=(VMEM, VMEM),
        scratch_shapes=[pltpu.VMEM((ways, 2 * length, here), BF16)],
        compiler_params=PARAMS,
        cost_estimate=pl.CostEstimate(flops=2**31, bytes_accessed=6 * 2**20, transcendentals=2**19),
        name="inside",
    )(place, decays, starts, *q_parts, *kv_parts)
    sparse_queries = exchange(sparse_query, after=(raw, *states))
    firsts = pl.pallas_call(
        first_kernel,
        out_shape=[jax.ShapeDtypeStruct((ways, length, here // 2), BF16)] * 2,
        in_specs=[VMEM] * (4 + len(states)) + [ANY],
        out_specs=[VMEM] * 2,
        compiler_params=PARAMS,
        name="first",
    )(raw, queries, decays, gain, *states, earlier_keys)
    earlier_firsts = [onward(x) for x in firsts]

    steps = blocks // STEP
    rows = STEP * BLK
    whole = pl.BlockSpec((tokens, here), lambda g: (0, 0))
    part = pl.BlockSpec((rows, here), lambda g: (g, 0))
    table = pl.BlockSpec((heads, rows, picks * BLK), lambda g: (0, g, 0))
    weights = pl.pallas_call(
        weights_kernel,
        out_shape=jax.ShapeDtypeStruct((heads, tokens, picks * BLK), BF16),
        grid=(steps,),
        in_specs=[SMEM, whole, whole, pl.BlockSpec((blocks, picks * BLK), lambda g: (0, 0)), part],
        out_specs=table,
        scratch_shapes=[
            pltpu.VMEM((2 * tokens, here), BF16),
            pltpu.VMEM((STEP, picks * BLK, here), BF16),
        ],
        compiler_params=PARAMS,
        cost_estimate=pl.CostEstimate(flops=2**31, bytes_accessed=8 * 2**20, transcendentals=2**21),
        name="weights",
    )(
        window,
        sparse_keys.reshape(tokens, here),
        earlier_keys.reshape(tokens, here),
        bias,
        sparse_queries.reshape(tokens, here),
    )
    order = (peers[:, None] * 2 + cores[None, :]).reshape(-1).astype(jnp.int32)
    some = here // 2
    whole = pl.BlockSpec((tokens, some), lambda g, *_: (0, 0))
    sums = []
    for half, (own, earlier) in enumerate(zip(firsts, earlier_firsts)):
        outs = pl.pallas_call(
            sum_kernel,
            out_shape=[jax.ShapeDtypeStruct((2, length, some), BF16)] * chips,
            grid_spec=pltpu.PrefetchScalarGridSpec(
                num_scalar_prefetch=2,
                grid=(ways,),
                in_specs=[
                    pl.BlockSpec((heads // 2, length, picks * BLK), lambda g, order, _, half=half: (half, order[g], 0)),
                    whole,
                    whole,
                ],
                out_specs=[
                    pl.BlockSpec((1, length, some), lambda g, *_, k=k: (jnp.clip(g - 2 * k, 0, 1), 0, 0))
                    for k in range(chips)
                ],
                scratch_shapes=[
                    pltpu.VMEM((2 * tokens, some), BF16),
                    pltpu.VMEM((length // BLK, picks * BLK, some), BF16),
                ],
            ),
            compiler_params=PARAMS,
            name="sum",
        )(order, window, weights, own.reshape(tokens, some), earlier.reshape(tokens, some))
        for k, out in enumerate(outs):
            if k:
                out = lax.ppermute(out, ("side", "inner"), [(i, i ^ (2 * k)) for i in range(ways)])
            sums += [out, swap(out)]
    return pl.pallas_call(
        join_kernel,
        out_shape=jax.ShapeDtypeStruct((length, model), BF16),
        grid=(1,),
        in_specs=[SMEM]
        + [pl.BlockSpec((1, length, some), lambda g, core=n % 2: (core, 0, 0)) for n in range(len(sums))],
        out_specs=pl.BlockSpec((length, model), lambda g: (0, 0)),
        compiler_params=PARAMS,
        name="join",
    )(columns, *sums)


def solution(mesh):
    spans, inner = mesh.devices.shape
    finer = Mesh(mesh.devices.reshape(spans // 2, 2, inner), ("group", "side", "inner"))
    rows = P(("group", "side", "inner"), None)
    placed = (rows,) * 5 + (P("inner", ("group", "side")), P("inner", None), P(("group", "side"), None))
    return jax.shard_map(local, mesh=finer, in_specs=placed, out_specs=rows, check_vma=False)
```

```python
import math

import jax
import jax.numpy as jnp
from jax import lax
from jax.experimental import pallas as pl
from jax.experimental.pallas import tpu as pltpu
from jax.sharding import Mesh
from jax.sharding import PartitionSpec as P

BLK = 64
STEP = 2
F32 = jnp.float32
BF16 = jnp.bfloat16
HIGHEST = lax.Precision.HIGHEST
VMEM = pl.BlockSpec(memory_space=pltpu.VMEM)
SMEM = pl.BlockSpec(memory_space=pltpu.SMEM)
ANY = pl.BlockSpec(memory_space=pl.ANY)
HBM = pl.BlockSpec(memory_space=pltpu.HBM)
PARAMS = pltpu.CompilerParams(vmem_limit_bytes=16 * 2**20)


def halves(x):
    high = x.astype(BF16)
    return high, (x - high.astype(F32)).astype(BF16)


def dot(a, b, dims):
    return lax.dot_general(a, b, (dims, ((), ())), preferred_element_type=F32)


def exact(a, b, dims):
    return lax.dot_general(a, b, (dims, ((), ())), precision=HIGHEST, preferred_element_type=F32)


def grid_of(shape):
    return lax.broadcasted_iota(jnp.int32, shape, 0), lax.broadcasted_iota(jnp.int32, shape, 1)


def summed_down(logs):
    length = logs.shape[1]
    row, col = grid_of((length, length))
    return exact((row >= col).astype(F32), logs, ((1,), (1,)))


def other_chunks(totals, chunks, later):
    count = totals.shape[1]
    row, col = grid_of((count, count))
    same = row // chunks == col // chunks
    taken = same & ((row > col) if later else (row < col))
    return exact(totals, taken.astype(F32), ((1,), (0,)))


def run_all(copies):
    for copy in copies:
        copy.start()
    for copy in copies:
        copy.wait()


def pieces_kernel(in_ref, *refs):
    out_ref, sem = refs[-2:]
    ways, _, here = out_ref.shape
    run_all([
        pltpu.make_async_copy(
            in_ref.at[:, pl.ds((d % (ways // 2) * 2 + d // (ways // 2)) * here, here)], out_ref.at[d], sem.at[d]
        )
        for d in range(ways)
    ])


def outward_kernel(count, columns_ref, *refs):
    ins, out_ref, sem = refs[:count], refs[-2], refs[-1]
    length, here = ins[0].shape[0], out_ref.shape[2]
    run_all([
        pltpu.make_async_copy(
            ref.at[:, pl.ds(pl.multiple_of(columns_ref[k, 1], 128), here)],
            out_ref.at[k, pl.ds(n * length, length), :],
            sem.at[k, n],
        )
        for k in range(out_ref.shape[0])
        for n, ref in enumerate(ins)
    ])


def thirds(x):
    first = x.astype(BF16).astype(F32)
    second = (x - first).astype(BF16).astype(F32)
    return first, second, x - first - second


def parcel_kernel(count, extra, columns_ref, place_ref, *refs):
    ins, got_ref, table_ref = refs[:count], refs[count], refs[count + 1]
    scratch = 2 if extra else 1
    chips = got_ref.shape[0]
    outs, sem = refs[-scratch - chips : -scratch], refs[-1]
    length, here = ins[0].shape[0], got_ref.shape[2]
    core = place_ref[1]
    copies = []
    for k, out_ref in enumerate(outs):
        start = pl.multiple_of(columns_ref[k, 0], 128)
        for n, ref in enumerate(ins):
            copies.append(
                pltpu.make_async_copy(
                    ref.at[:, pl.ds(start, here)], out_ref.at[core, pl.ds(n * length, length), :], sem.at[k, n]
                )
            )
        copies.append(
            pltpu.make_async_copy(
                got_ref.at[k], out_ref.at[1 - core, pl.ds(0, count * length), :], sem.at[k, count]
            )
        )
    if extra:
        rows_ref = refs[-2]
        parts = jnp.concatenate(thirds(table_ref[...]), 0)
        if extra > parts.shape[0]:
            parts = jnp.concatenate([parts, jnp.zeros((extra - parts.shape[0], here), F32)], 0)
        for n in range(2):
            rows_ref[n] = parts.astype(BF16)
        copies.append(
            pltpu.make_async_copy(
                rows_ref, outs[chips // 2].at[:, pl.ds(count * length, extra), :], sem.at[0, count + 1]
            )
        )
    run_all(copies)


def gather_chunks(place_ref, refs, out_ref):
    for k, ref in enumerate(refs):
        chip = jnp.bitwise_xor(place_ref[0], k)
        out_ref[pl.ds(pl.multiple_of(2 * chip, 2), 2)] = ref[:, : out_ref.shape[1], :]


def state_kernel(place_ref, table_ref, *refs):
    parts, (sent_ref, start_ref, decay_ref, other_ref, kv_ref) = refs[:-5], refs[-5:]
    heads, width = sent_ref.shape[0], sent_ref.shape[2]
    chunks = kv_ref.shape[0]
    length = kv_ref.shape[1] // 2
    gather_chunks(place_ref, parts, kv_ref)
    size, here = table_ref.shape
    got = parts[len(parts) // 2][0, 2 * length :, :].astype(F32)
    mine, theirs = table_ref[...], got[:size] + got[size : 2 * size] + got[2 * size : 3 * size]
    leads = place_ref[2] == 0
    spans = (jnp.where(leads, mine, theirs), jnp.where(leads, theirs, mine))
    span = size * here // (heads + 1)
    for n, table in enumerate(spans):
        for h in range(heads):
            for t in range(chunks // 2):
                row, lane = divmod(h * span + t * length, here)
                at = h * chunks + n * (chunks // 2) + t
                decay_ref[at : at + 1, :] = table[row : row + 1, lane : lane + length]
        other_ref[n] = table[size - span // here :, :]
    down = summed_down(jnp.log(decay_ref[...]))
    totals = down[length - 1 : length, :]
    left = jnp.exp(totals - down)
    kept = jnp.exp(totals)
    factors = jnp.exp(totals + other_chunks(totals, chunks, True))
    place = lax.broadcasted_iota(jnp.int32, (16, width), 0)
    for h in range(heads):
        columns = slice(h * width, (h + 1) * width)
        state = jnp.zeros((width, width), F32)
        for c in range(chunks):
            at = h * chunks + c
            if c:
                high, low = halves(state)
                start_ref[h, c, :width, :] = high
                start_ref[h, c, width:, :] = low
            keys = kv_ref[c, :length, columns].astype(F32)
            values = kv_ref[c, length:, columns]
            high, low = halves(keys * left[:, at : at + 1])
            state = kept[:, at : at + 1] * state + dot(
                jnp.concatenate([high, low], 0), jnp.concatenate([values, values], 0), ((0,), (0,))
            )
        sent_ref[h, :width, :] = state.astype(BF16)
        factor = factors[:, h * chunks : h * chunks + 1]
        first, second, third = thirds(factor)
        sent_ref[h, width:, :] = jnp.where(
            place == 0, first, jnp.where(place == 1, second, jnp.where(place == 2, third, 0.0))
        ).astype(BF16)


def inside_kernel(count, place_ref, decay_ref, start_ref, *refs):
    q_parts, kv_parts, (raw_ref, q_ref, kv_ref) = refs[:count], refs[count : 2 * count], refs[2 * count :]
    chunks, length, here = q_ref.shape
    heads = decay_ref.shape[0] // chunks
    width = here // heads
    gather_chunks(place_ref, q_parts, q_ref)
    gather_chunks(place_ref, kv_parts, kv_ref)
    logs = jnp.log(decay_ref[...])
    row, col = grid_of((length, length))
    along = exact(logs, (row <= col).astype(F32), ((1,), (0,)))
    down = summed_down(logs)
    lifts = jnp.exp(down)
    causal = row >= col
    for h in range(heads):
        columns = slice(h * width, (h + 1) * width)
        for c in range(chunks):
            at = h * chunks + c
            queries = q_ref[c, :, columns]
            keys = kv_ref[c, :length, columns]
            values = kv_ref[c, length:, columns]
            gap = jnp.where(causal, down[:, at : at + 1] - along[at : at + 1, :], 0.0)
            weights = jnp.where(causal, jnp.exp(gap), 0.0) * dot(queries, keys, ((1,), (1,)))
            raw = dot(jnp.concatenate(halves(weights), 1), jnp.concatenate([values, values], 0), ((1,), (0,)))
            if c:
                raw = raw + lifts[:, at : at + 1] * dot(
                    jnp.concatenate([queries, queries], 1), start_ref[h, c], ((1,), (0,))
                )
            raw_ref[c, :, columns] = raw


def first_kernel(raw_ref, q_ref, decay_ref, gain_ref, *refs):
    earlier, outs = refs[:-3], refs[-2:]
    chunks, length, here = q_ref.shape
    heads, width = gain_ref.shape
    down = summed_down(jnp.log(decay_ref[...]))
    lifts = jnp.exp(down + other_chunks(down[length - 1 : length, :], chunks, False))
    for h in range(heads):
        columns = slice(h * width, (h + 1) * width)
        carried = jnp.zeros((width, width), F32)
        factor = jnp.ones((1, 1), F32)
        for ref in earlier:
            carried = carried + factor * ref[h, :width, :].astype(F32)
            parts = ref[h, width:, :].astype(F32)
            factor = factor * (parts[0:1, 0:1] + parts[1:2, 0:1] + parts[2:3, 0:1])
        both = jnp.concatenate(halves(carried), 0)
        gain = gain_ref[h : h + 1, :]
        place = h % (heads // 2)
        for c in range(chunks):
            at = h * chunks + c
            queries = q_ref[c, :, columns]
            outside = dot(jnp.concatenate([queries, queries], 1), both, ((1,), (0,)))
            raw = raw_ref[c, :, columns] + lifts[:, at : at + 1] * outside
            scale = lax.rsqrt(jnp.mean(raw * raw, axis=-1, keepdims=True) + 1e-06)
            outs[h // (heads // 2)][c, :, place * width : (place + 1) * width] = (raw * scale * gain).astype(BF16)


def pick(window_ref, b, source_ref, picked_ref):
    for j in range(picked_ref.shape[0] // BLK):
        start = pl.multiple_of(window_ref[b, j] * BLK, BLK)
        picked_ref[j * BLK : (j + 1) * BLK, :] = source_ref[pl.ds(start, BLK), :]


def weights_kernel(window_ref, own_ref, earlier_ref, bias_ref, q_ref, out_ref, keys_ref, picked_ref):
    tokens, here = own_ref.shape
    heads = out_ref.shape[0]
    width = here // heads
    picks = picked_ref.shape[1] // BLK
    group = pl.program_id(0)

    @pl.when(group == 0)
    def _():
        keys_ref[:tokens, :] = earlier_ref[...]
        keys_ref[tokens:, :] = own_ref[...]

    row, col = grid_of((BLK, picks * BLK))
    causal = jnp.where((col >= BLK) | (col <= row), 0.0, -1e30)
    scale = 1.0 / math.sqrt(width)
    for t in range(STEP):
        b = group * STEP + t
        pick(window_ref, b, keys_ref, picked_ref.at[t])
        bias = causal + bias_ref[pl.ds(b, 1), :]
        for h in range(heads):
            columns = slice(h * width, (h + 1) * width)
            scores = dot(q_ref[t * BLK : (t + 1) * BLK, columns], picked_ref[t, :, columns], ((1,), (1,))) * scale
            scores = scores + bias
            probs = jnp.exp(scores - jnp.max(scores, axis=-1, keepdims=True))
            share = 1.0 / jnp.sum(probs, axis=-1, keepdims=True)
            out_ref[h, t * BLK : (t + 1) * BLK, :] = (probs * share).astype(BF16)


def sum_kernel(order_ref, window_ref, weights_ref, own_ref, earlier_ref, *refs):
    outs, values_ref, picked_ref = refs[:-2], refs[-2], refs[-1]
    tokens, here = own_ref.shape
    heads, length, _ = weights_ref.shape
    width = here // heads
    step = pl.program_id(0)

    @pl.when(step == 0)
    def _():
        values_ref[:tokens, :] = earlier_ref[...]
        values_ref[tokens:, :] = own_ref[...]

    results = []
    for t in range(length // BLK):
        b = order_ref[step] * (length // BLK) + t
        pick(window_ref, b, values_ref, picked_ref.at[t])
        rows = pl.ds(pl.multiple_of(b * BLK, BLK), BLK)
        for h in range(heads):
            columns = slice(h * width, (h + 1) * width)
            second = dot(weights_ref[h, t * BLK : (t + 1) * BLK, :], picked_ref[t, :, columns], ((1,), (0,)))
            results.append((t, columns, (own_ref[rows, columns].astype(F32) + second).astype(BF16)))
    for k, out_ref in enumerate(outs):

        @pl.when(step // 2 == k)
        def _(out_ref=out_ref):
            for t, columns, result in results:
                out_ref[0, t * BLK : (t + 1) * BLK, columns] = result


def join_kernel(columns_ref, *refs):
    parts, out_ref = refs[:-1], refs[-1]
    here = parts[0].shape[2]
    chips = columns_ref.shape[0]
    for n, ref in enumerate(parts):
        half, k, core = n // (2 * chips), n // 2 % chips, n % 2
        start = pl.multiple_of(columns_ref[k, core] + half * here, 128)
        out_ref[:, pl.ds(start, here)] = ref[0]


def local(lin_query, lin_key, lin_value, sparse_query, sparse_key, decay, norm_gain, block_pattern):
    groups, inner = lax.axis_size("group"), lax.axis_size("inner")
    level, side, index = lax.axis_index("group"), lax.axis_index("side"), lax.axis_index("inner")
    ways = 2 * inner
    chips = ways // 2
    length, model = lin_query.shape
    width = norm_gain.shape[1]
    heads = norm_gain.shape[0] // 2
    here = heads * width
    tokens = ways * length
    blocks = tokens // BLK
    picks = block_pattern.shape[1]

    chip, core = side * (inner // 2) + index // 2, index % 2
    place = jnp.stack([chip, core, side]).astype(jnp.int32)
    peers = jnp.bitwise_xor(chip, jnp.arange(chips, dtype=jnp.int32))
    cores = jnp.stack([core, 1 - core])
    indices = (peers % (inner // 2))[:, None] * 2 + cores[None, :]
    columns = ((indices * 2 + (peers // (inner // 2))[:, None]) * here).astype(jnp.int32)

    def swap(x):
        return lax.ppermute(x, ("side", "inner"), [(i, i ^ 1) for i in range(ways)])

    def spread(*arrays, table=None, after=(), first=()):
        rows = len(arrays) * length
        extra = 0 if table is None else -(-3 * table.shape[0] // 16) * 16
        after = after if table is None else (table, *after)
        out = pl.pallas_call(
            lambda *refs: outward_kernel(len(arrays), *refs),
            out_shape=pltpu.HBM((chips, rows, here), BF16),
            in_specs=[SMEM] + [VMEM] * len(arrays) + [ANY] * len(first),
            out_specs=HBM,
            scratch_shapes=[pltpu.SemaphoreType.DMA((chips, len(arrays)))],
            compiler_params=PARAMS,
            name="outward",
        )(columns, *arrays, *first)
        parcels = pl.pallas_call(
            lambda *refs: parcel_kernel(len(arrays), extra, *refs),
            out_shape=[
                pltpu.HBM((2, rows + (extra if k == chips // 2 else 0), here), BF16) for k in range(chips)
            ],
            in_specs=[SMEM, SMEM] + [VMEM] * (len(arrays) + 1) + [VMEM] * bool(extra) + [ANY] * (len(after) - bool(extra)),
            out_specs=[HBM] * chips,
            scratch_shapes=[pltpu.VMEM((2, extra, here), BF16)] * bool(extra)
            + [pltpu.SemaphoreType.DMA((chips, len(arrays) + 2))],
            compiler_params=PARAMS,
            name="parcels",
        )(columns, place, *arrays, swap(out), *after)
        return parcels, [parcels[0]] + [
            lax.ppermute(x, ("side", "inner"), [(i, i ^ (2 * k)) for i in range(ways)])
            for k, x in enumerate(parcels)
            if k
        ]

    def exchange(x, after=()):
        pieces = pl.pallas_call(
            pieces_kernel,
            out_shape=pltpu.HBM((ways, length, here), BF16),
            in_specs=[VMEM] + [ANY] * len(after),
            out_specs=HBM,
            scratch_shapes=[pltpu.SemaphoreType.DMA((ways,))],
            compiler_params=PARAMS,
            name="pieces",
        )(x, *after)
        return pieces, lax.all_to_all(pieces, ("side", "inner"), split_axis=0, concat_axis=0, tiled=True)

    def onward(x, steps=1):
        return lax.ppermute(x, "group", [(i, i + steps) for i in range(groups - steps)])

    span = decay.shape[1]
    flat = block_pattern.reshape(1, -1).astype(F32)
    flat = jnp.pad(flat, ((0, 0), (0, span - flat.shape[1])))

    def table(first_head):
        return jnp.concatenate([lax.dynamic_slice_in_dim(decay, first_head, heads, 0), flat], 0).reshape(-1, here)

    mine = table(side * heads)
    gain = lax.dynamic_slice_in_dim(norm_gain, side * heads, heads, 0)

    pieces, sparse_keys = exchange(sparse_key)
    parcels, kv_parts = spread(lin_key, lin_value, table=table((1 - side) * heads), first=(pieces,))
    _, q_parts = spread(lin_query, after=kv_parts[1:3])
    earlier_keys = onward(sparse_keys)

    sent, starts, decays, others = pl.pallas_call(
        state_kernel,
        out_shape=(
            jax.ShapeDtypeStruct((heads, width + 16, width), BF16),
            jax.ShapeDtypeStruct((heads, ways, 2 * width, width), BF16),
            jax.ShapeDtypeStruct((heads * ways, length), F32),
            jax.ShapeDtypeStruct((2, span // here, here), F32),
        ),
        in_specs=[SMEM, VMEM] + [VMEM] * chips,
        out_specs=(VMEM,) * 4,
        scratch_shapes=[pltpu.VMEM((ways, 2 * length, here), BF16)],
        compiler_params=PARAMS,
        name="state",
    )(place, mine, *kv_parts)
    pattern = others.reshape(2, span)[:, : block_pattern.size].reshape(blocks, picks).astype(jnp.int32)
    window = jnp.where(pattern >= 0, pattern - (level - 1) * blocks, 0)
    bias = jnp.repeat(jnp.where(pattern >= 0, 0.0, -1e30).astype(F32), BLK, axis=1)
    states = [onward(sent, steps) for steps in range(1, groups)]
    raw, queries = pl.pallas_call(
        lambda *refs: inside_kernel(chips, *refs),
        out_shape=(
            jax.ShapeDtypeStruct((ways, length, here), F32),
            jax.ShapeDtypeStruct((ways, length, here), BF16),
        ),
        in_specs=[SMEM, VMEM, VMEM] + [VMEM] * (2 * chips),
        out_specs=(VMEM, VMEM),
        scratch_shapes=[pltpu.VMEM((ways, 2 * length, here), BF16)],
        compiler_params=PARAMS,
        cost_estimate=pl.CostEstimate(flops=2**31, bytes_accessed=6 * 2**20, transcendentals=2**19),
        name="inside",
    )(place, decays, starts, *q_parts, *kv_parts)
    _, sparse_queries = exchange(sparse_query, after=(raw, *states))
    firsts = pl.pallas_call(
        first_kernel,
        out_shape=[jax.ShapeDtypeStruct((ways, length, here // 2), BF16)] * 2,
        in_specs=[VMEM] * (4 + len(states)) + [ANY],
        out_specs=[VMEM] * 2,
        compiler_params=PARAMS,
        name="first",
    )(raw, queries, decays, gain, *states, earlier_keys)
    earlier_firsts = [onward(x) for x in firsts]

    steps = blocks // STEP
    rows = STEP * BLK
    whole = pl.BlockSpec((tokens, here), lambda g: (0, 0))
    part = pl.BlockSpec((rows, here), lambda g: (g, 0))
    table = pl.BlockSpec((heads, rows, picks * BLK), lambda g: (0, g, 0))
    weights = pl.pallas_call(
        weights_kernel,
        out_shape=jax.ShapeDtypeStruct((heads, tokens, picks * BLK), BF16),
        grid=(steps,),
        in_specs=[SMEM, whole, whole, pl.BlockSpec((blocks, picks * BLK), lambda g: (0, 0)), part],
        out_specs=table,
        scratch_shapes=[
            pltpu.VMEM((2 * tokens, here), BF16),
            pltpu.VMEM((STEP, picks * BLK, here), BF16),
        ],
        compiler_params=PARAMS,
        cost_estimate=pl.CostEstimate(flops=2**31, bytes_accessed=8 * 2**20, transcendentals=2**21),
        name="weights",
    )(
        window,
        sparse_keys.reshape(tokens, here),
        earlier_keys.reshape(tokens, here),
        bias,
        sparse_queries.reshape(tokens, here),
    )
    order = (peers[:, None] * 2 + cores[None, :]).reshape(-1).astype(jnp.int32)
    some = here // 2
    whole = pl.BlockSpec((tokens, some), lambda g, *_: (0, 0))
    sums = []
    for half, (own, earlier) in enumerate(zip(firsts, earlier_firsts)):
        outs = pl.pallas_call(
            sum_kernel,
            out_shape=[jax.ShapeDtypeStruct((2, length, some), BF16)] * chips,
            grid_spec=pltpu.PrefetchScalarGridSpec(
                num_scalar_prefetch=2,
                grid=(ways,),
                in_specs=[
                    pl.BlockSpec((heads // 2, length, picks * BLK), lambda g, order, _, half=half: (half, order[g], 0)),
                    whole,
                    whole,
                ],
                out_specs=[
                    pl.BlockSpec((1, length, some), lambda g, *_, k=k: (jnp.clip(g - 2 * k, 0, 1), 0, 0))
                    for k in range(chips)
                ],
                scratch_shapes=[
                    pltpu.VMEM((2 * tokens, some), BF16),
                    pltpu.VMEM((length // BLK, picks * BLK, some), BF16),
                ],
            ),
            compiler_params=PARAMS,
            name="sum",
        )(order, window, weights, own.reshape(tokens, some), earlier.reshape(tokens, some))
        for k, out in enumerate(outs):
            if k:
                out = lax.ppermute(out, ("side", "inner"), [(i, i ^ (2 * k)) for i in range(ways)])
            sums += [out, swap(out)]
    return pl.pallas_call(
        join_kernel,
        out_shape=jax.ShapeDtypeStruct((length, model), BF16),
        grid=(1,),
        in_specs=[SMEM]
        + [pl.BlockSpec((1, length, some), lambda g, core=n % 2: (core, 0, 0)) for n in range(len(sums))],
        out_specs=pl.BlockSpec((length, model), lambda g: (0, 0)),
        compiler_params=PARAMS,
        name="join",
    )(columns, *sums)


def solution(mesh):
    spans, inner = mesh.devices.shape
    finer = Mesh(mesh.devices.reshape(spans // 2, 2, inner), ("group", "side", "inner"))
    rows = P(("group", "side", "inner"), None)
    placed = (rows,) * 5 + (P("inner", ("group", "side")), P("inner", None), P(("group", "side"), None))
    return jax.shard_map(local, mesh=finer, in_specs=placed, out_specs=rows, check_vma=False)
```

```python
import math

import jax
import jax.numpy as jnp
from jax import lax
from jax.experimental import pallas as pl
from jax.experimental.pallas import tpu as pltpu
from jax.sharding import Mesh
from jax.sharding import PartitionSpec as P

BLK = 64
STEP = 2
F32 = jnp.float32
BF16 = jnp.bfloat16
HIGHEST = lax.Precision.HIGHEST
VMEM = pl.BlockSpec(memory_space=pltpu.VMEM)
SMEM = pl.BlockSpec(memory_space=pltpu.SMEM)
ANY = pl.BlockSpec(memory_space=pl.ANY)
HBM = pl.BlockSpec(memory_space=pltpu.HBM)
PARAMS = pltpu.CompilerParams(vmem_limit_bytes=16 * 2**20)


def halves(x):
    high = x.astype(BF16)
    return high, (x - high.astype(F32)).astype(BF16)


def dot(a, b, dims):
    return lax.dot_general(a, b, (dims, ((), ())), preferred_element_type=F32)


def exact(a, b, dims):
    return lax.dot_general(a, b, (dims, ((), ())), precision=HIGHEST, preferred_element_type=F32)


def grid_of(shape):
    return lax.broadcasted_iota(jnp.int32, shape, 0), lax.broadcasted_iota(jnp.int32, shape, 1)


def summed_down(logs):
    length = logs.shape[1]
    row, col = grid_of((length, length))
    return exact((row >= col).astype(F32), logs, ((1,), (1,)))


def other_chunks(totals, chunks, later):
    count = totals.shape[1]
    row, col = grid_of((count, count))
    same = row // chunks == col // chunks
    taken = same & ((row > col) if later else (row < col))
    return exact(totals, taken.astype(F32), ((1,), (0,)))


def run_all(copies):
    for copy in copies:
        copy.start()
    for copy in copies:
        copy.wait()


def pieces_kernel(in_ref, *refs):
    out_ref, sem = refs[-2:]
    ways, _, here = out_ref.shape
    run_all([
        pltpu.make_async_copy(
            in_ref.at[:, pl.ds((d % (ways // 2) * 2 + d // (ways // 2)) * here, here)], out_ref.at[d], sem.at[d]
        )
        for d in range(ways)
    ])


def outward_kernel(count, columns_ref, *refs):
    ins, out_ref, sem = refs[:count], refs[-2], refs[-1]
    length, here = ins[0].shape[0], out_ref.shape[2]
    run_all([
        pltpu.make_async_copy(
            ref.at[:, pl.ds(pl.multiple_of(columns_ref[k, 1], 128), here)],
            out_ref.at[k, pl.ds(n * length, length), :],
            sem.at[k, n],
        )
        for k in range(out_ref.shape[0])
        for n, ref in enumerate(ins)
    ])


def thirds(x):
    first = x.astype(BF16).astype(F32)
    second = (x - first).astype(BF16).astype(F32)
    return first, second, x - first - second


def parcel_kernel(count, extra, columns_ref, place_ref, *refs):
    ins, got_ref, table_ref = refs[:count], refs[count], refs[count + 1]
    scratch = 2 if extra else 1
    chips = got_ref.shape[0]
    outs, sem = refs[-scratch - chips : -scratch], refs[-1]
    length, here = ins[0].shape[0], got_ref.shape[2]
    core = place_ref[1]
    copies = []
    for k, out_ref in enumerate(outs):
        start = pl.multiple_of(columns_ref[k, 0], 128)
        for n, ref in enumerate(ins):
            copies.append(
                pltpu.make_async_copy(
                    ref.at[:, pl.ds(start, here)], out_ref.at[core, pl.ds(n * length, length), :], sem.at[k, n]
                )
            )
        copies.append(
            pltpu.make_async_copy(
                got_ref.at[k], out_ref.at[1 - core, pl.ds(0, count * length), :], sem.at[k, count]
            )
        )
    if extra:
        rows_ref = refs[-2]
        parts = jnp.concatenate(thirds(table_ref[...]), 0)
        if extra > parts.shape[0]:
            parts = jnp.concatenate([parts, jnp.zeros((extra - parts.shape[0], here), F32)], 0)
        for n in range(2):
            rows_ref[n] = parts.astype(BF16)
        copies.append(
            pltpu.make_async_copy(
                rows_ref, outs[chips // 2].at[:, pl.ds(count * length, extra), :], sem.at[0, count + 1]
            )
        )
    run_all(copies)


def gather_chunks(place_ref, refs, out_ref):
    for k, ref in enumerate(refs):
        chip = jnp.bitwise_xor(place_ref[0], k)
        out_ref[pl.ds(pl.multiple_of(2 * chip, 2), 2)] = ref[:, : out_ref.shape[1], :]


def state_kernel(place_ref, table_ref, *refs):
    parts, (sent_ref, start_ref, decay_ref, other_ref, kv_ref) = refs[:-5], refs[-5:]
    heads, width = sent_ref.shape[0], sent_ref.shape[2]
    chunks = kv_ref.shape[0]
    length = kv_ref.shape[1] // 2
    gather_chunks(place_ref, parts, kv_ref)
    size, here = table_ref.shape
    got = parts[len(parts) // 2][0, 2 * length :, :].astype(F32)
    mine, theirs = table_ref[...], got[:size] + got[size : 2 * size] + got[2 * size : 3 * size]
    leads = place_ref[2] == 0
    spans = (jnp.where(leads, mine, theirs), jnp.where(leads, theirs, mine))
    span = size * here // (heads + 1)
    for n, table in enumerate(spans):
        for h in range(heads):
            for t in range(chunks // 2):
                row, lane = divmod(h * span + t * length, here)
                at = h * chunks + n * (chunks // 2) + t
                decay_ref[at : at + 1, :] = table[row : row + 1, lane : lane + length]
        other_ref[n] = table[size - span // here :, :]
    down = summed_down(jnp.log(decay_ref[...]))
    totals = down[length - 1 : length, :]
    left = jnp.exp(totals - down)
    kept = jnp.exp(totals)
    factors = jnp.exp(totals + other_chunks(totals, chunks, True))
    place = lax.broadcasted_iota(jnp.int32, (16, width), 0)
    for h in range(heads):
        columns = slice(h * width, (h + 1) * width)
        state = jnp.zeros((width, width), F32)
        for c in range(chunks):
            at = h * chunks + c
            if c:
                high, low = halves(state)
                start_ref[h, c, :width, :] = high
                start_ref[h, c, width:, :] = low
            keys = kv_ref[c, :length, columns].astype(F32)
            values = kv_ref[c, length:, columns]
            high, low = halves(keys * left[:, at : at + 1])
            state = kept[:, at : at + 1] * state + dot(
                jnp.concatenate([high, low], 0), jnp.concatenate([values, values], 0), ((0,), (0,))
            )
        sent_ref[h, :width, :] = state.astype(BF16)
        factor = factors[:, h * chunks : h * chunks + 1]
        first, second, third = thirds(factor)
        sent_ref[h, width:, :] = jnp.where(
            place == 0, first, jnp.where(place == 1, second, jnp.where(place == 2, third, 0.0))
        ).astype(BF16)


def inside_kernel(count, place_ref, decay_ref, start_ref, *refs):
    q_parts, kv_parts, (raw_ref, q_ref, kv_ref) = refs[:count], refs[count : 2 * count], refs[2 * count :]
    chunks, length, here = q_ref.shape
    heads = decay_ref.shape[0] // chunks
    width = here // heads
    gather_chunks(place_ref, q_parts, q_ref)
    gather_chunks(place_ref, kv_parts, kv_ref)
    logs = jnp.log(decay_ref[...])
    row, col = grid_of((length, length))
    along = exact(logs, (row <= col).astype(F32), ((1,), (0,)))
    down = summed_down(logs)
    lifts = jnp.exp(down)
    causal = row >= col
    for h in range(heads):
        columns = slice(h * width, (h + 1) * width)
        for c in range(chunks):
            at = h * chunks + c
            queries = q_ref[c, :, columns]
            keys = kv_ref[c, :length, columns]
            values = kv_ref[c, length:, columns]
            gap = jnp.where(causal, down[:, at : at + 1] - along[at : at + 1, :], 0.0)
            weights = jnp.where(causal, jnp.exp(gap), 0.0) * dot(queries, keys, ((1,), (1,)))
            raw = dot(jnp.concatenate(halves(weights), 1), jnp.concatenate([values, values], 0), ((1,), (0,)))
            if c:
                raw = raw + lifts[:, at : at + 1] * dot(
                    jnp.concatenate([queries, queries], 1), start_ref[h, c], ((1,), (0,))
                )
            raw_ref[c, :, columns] = raw


def first_kernel(raw_ref, q_ref, decay_ref, gain_ref, *refs):
    earlier, outs, (made_ref, sem) = refs[:-5], refs[-4:-2], refs[-2:]
    chunks, length, here = q_ref.shape
    heads, width = gain_ref.shape
    down = summed_down(jnp.log(decay_ref[...]))
    lifts = jnp.exp(down + other_chunks(down[length - 1 : length, :], chunks, False))
    copies = []
    for h in range(heads):
        columns = slice(h * width, (h + 1) * width)
        carried = jnp.zeros((width, width), F32)
        factor = jnp.ones((1, 1), F32)
        for ref in earlier:
            carried = carried + factor * ref[h, :width, :].astype(F32)
            parts = ref[h, width:, :].astype(F32)
            factor = factor * (parts[0:1, 0:1] + parts[1:2, 0:1] + parts[2:3, 0:1])
        both = jnp.concatenate(halves(carried), 0)
        gain = gain_ref[h : h + 1, :]
        half, place = divmod(h, heads // 2)
        for c in range(chunks):
            at = h * chunks + c
            queries = q_ref[c, :, columns]
            outside = dot(jnp.concatenate([queries, queries], 1), both, ((1,), (0,)))
            raw = raw_ref[c, :, columns] + lifts[:, at : at + 1] * outside
            scale = lax.rsqrt(jnp.mean(raw * raw, axis=-1, keepdims=True) + 1e-06)
            made_ref[half, c, :, place * width : (place + 1) * width] = (raw * scale * gain).astype(BF16)
        if place == heads // 2 - 1:
            copies.append(pltpu.make_async_copy(made_ref.at[half], outs[half], sem.at[half]))
            copies[-1].start()
    for copy in copies:
        copy.wait()


def pick(window_ref, b, source_ref, picked_ref):
    for j in range(picked_ref.shape[0] // BLK):
        start = pl.multiple_of(window_ref[b, j] * BLK, BLK)
        picked_ref[j * BLK : (j + 1) * BLK, :] = source_ref[pl.ds(start, BLK), :]


def weights_kernel(window_ref, own_ref, earlier_ref, bias_ref, q_ref, out_ref, keys_ref, picked_ref):
    tokens, here = own_ref.shape
    heads = out_ref.shape[0]
    width = here // heads
    picks = picked_ref.shape[1] // BLK
    group = pl.program_id(0)

    @pl.when(group == 0)
    def _():
        keys_ref[:tokens, :] = earlier_ref[...]
        keys_ref[tokens:, :] = own_ref[...]

    row, col = grid_of((BLK, picks * BLK))
    causal = jnp.where((col >= BLK) | (col <= row), 0.0, -1e30)
    scale = 1.0 / math.sqrt(width)
    for t in range(STEP):
        b = group * STEP + t
        pick(window_ref, b, keys_ref, picked_ref.at[t])
        bias = causal + bias_ref[pl.ds(b, 1), :]
        for h in range(heads):
            columns = slice(h * width, (h + 1) * width)
            scores = dot(q_ref[t * BLK : (t + 1) * BLK, columns], picked_ref[t, :, columns], ((1,), (1,))) * scale
            scores = scores + bias
            probs = jnp.exp(scores - jnp.max(scores, axis=-1, keepdims=True))
            share = 1.0 / jnp.sum(probs, axis=-1, keepdims=True)
            out_ref[h, t * BLK : (t + 1) * BLK, :] = (probs * share).astype(BF16)


def sum_kernel(order_ref, window_ref, weights_ref, own_ref, earlier_ref, *refs):
    outs, values_ref, picked_ref = refs[:-2], refs[-2], refs[-1]
    tokens, here = own_ref.shape
    heads, length, _ = weights_ref.shape
    width = here // heads
    step = pl.program_id(0)

    @pl.when(step == 0)
    def _():
        values_ref[:tokens, :] = earlier_ref[...]
        values_ref[tokens:, :] = own_ref[...]

    results = []
    for t in range(length // BLK):
        b = order_ref[step] * (length // BLK) + t
        pick(window_ref, b, values_ref, picked_ref.at[t])
        rows = pl.ds(pl.multiple_of(b * BLK, BLK), BLK)
        for h in range(heads):
            columns = slice(h * width, (h + 1) * width)
            second = dot(weights_ref[h, t * BLK : (t + 1) * BLK, :], picked_ref[t, :, columns], ((1,), (0,)))
            results.append((t, columns, (own_ref[rows, columns].astype(F32) + second).astype(BF16)))
    for k, out_ref in enumerate(outs):

        @pl.when(step // 2 == k)
        def _(out_ref=out_ref):
            for t, columns, result in results:
                out_ref[0, t * BLK : (t + 1) * BLK, columns] = result


def join_kernel(columns_ref, *refs):
    parts, out_ref = refs[:-1], refs[-1]
    here = parts[0].shape[2]
    chips = columns_ref.shape[0]
    for n, ref in enumerate(parts):
        half, k, core = n // (2 * chips), n // 2 % chips, n % 2
        start = pl.multiple_of(columns_ref[k, core] + half * here, 128)
        out_ref[:, pl.ds(start, here)] = ref[0]


def local(lin_query, lin_key, lin_value, sparse_query, sparse_key, decay, norm_gain, block_pattern):
    groups, inner = lax.axis_size("group"), lax.axis_size("inner")
    level, side, index = lax.axis_index("group"), lax.axis_index("side"), lax.axis_index("inner")
    ways = 2 * inner
    chips = ways // 2
    length, model = lin_query.shape
    width = norm_gain.shape[1]
    heads = norm_gain.shape[0] // 2
    here = heads * width
    tokens = ways * length
    blocks = tokens // BLK
    picks = block_pattern.shape[1]

    chip, core = side * (inner // 2) + index // 2, index % 2
    place = jnp.stack([chip, core, side]).astype(jnp.int32)
    peers = jnp.bitwise_xor(chip, jnp.arange(chips, dtype=jnp.int32))
    cores = jnp.stack([core, 1 - core])
    indices = (peers % (inner // 2))[:, None] * 2 + cores[None, :]
    columns = ((indices * 2 + (peers // (inner // 2))[:, None]) * here).astype(jnp.int32)

    def swap(x):
        return lax.ppermute(x, ("side", "inner"), [(i, i ^ 1) for i in range(ways)])

    def spread(*arrays, table=None, after=(), first=()):
        rows = len(arrays) * length
        extra = 0 if table is None else -(-3 * table.shape[0] // 16) * 16
        after = after if table is None else (table, *after)
        out = pl.pallas_call(
            lambda *refs: outward_kernel(len(arrays), *refs),
            out_shape=pltpu.HBM((chips, rows, here), BF16),
            in_specs=[SMEM] + [VMEM] * len(arrays) + [ANY] * len(first),
            out_specs=HBM,
            scratch_shapes=[pltpu.SemaphoreType.DMA((chips, len(arrays)))],
            compiler_params=PARAMS,
            name="outward",
        )(columns, *arrays, *first)
        parcels = pl.pallas_call(
            lambda *refs: parcel_kernel(len(arrays), extra, *refs),
            out_shape=[
                pltpu.HBM((2, rows + (extra if k == chips // 2 else 0), here), BF16) for k in range(chips)
            ],
            in_specs=[SMEM, SMEM] + [VMEM] * (len(arrays) + 1) + [VMEM] * bool(extra) + [ANY] * (len(after) - bool(extra)),
            out_specs=[HBM] * chips,
            scratch_shapes=[pltpu.VMEM((2, extra, here), BF16)] * bool(extra)
            + [pltpu.SemaphoreType.DMA((chips, len(arrays) + 2))],
            compiler_params=PARAMS,
            name="parcels",
        )(columns, place, *arrays, swap(out), *after)
        return parcels, [parcels[0]] + [
            lax.ppermute(x, ("side", "inner"), [(i, i ^ (2 * k)) for i in range(ways)])
            for k, x in enumerate(parcels)
            if k
        ]

    def exchange(x, after=()):
        pieces = pl.pallas_call(
            pieces_kernel,
            out_shape=pltpu.HBM((ways, length, here), BF16),
            in_specs=[VMEM] + [ANY] * len(after),
            out_specs=HBM,
            scratch_shapes=[pltpu.SemaphoreType.DMA((ways,))],
            compiler_params=PARAMS,
            name="pieces",
        )(x, *after)
        return pieces, lax.all_to_all(pieces, ("side", "inner"), split_axis=0, concat_axis=0, tiled=True)

    def onward(x, steps=1):
        return lax.ppermute(x, "group", [(i, i + steps) for i in range(groups - steps)])

    span = decay.shape[1]
    flat = block_pattern.reshape(1, -1).astype(F32)
    flat = jnp.pad(flat, ((0, 0), (0, span - flat.shape[1])))

    def table(first_head):
        return jnp.concatenate([lax.dynamic_slice_in_dim(decay, first_head, heads, 0), flat], 0).reshape(-1, here)

    mine = table(side * heads)
    gain = lax.dynamic_slice_in_dim(norm_gain, side * heads, heads, 0)

    pieces, sparse_keys = exchange(sparse_key)
    parcels, kv_parts = spread(lin_key, lin_value, table=table((1 - side) * heads), first=(pieces,))
    _, q_parts = spread(lin_query, after=kv_parts[1:3])
    earlier_keys = onward(sparse_keys)

    sent, starts, decays, others = pl.pallas_call(
        state_kernel,
        out_shape=(
            jax.ShapeDtypeStruct((heads, width + 16, width), BF16),
            jax.ShapeDtypeStruct((heads, ways, 2 * width, width), BF16),
            jax.ShapeDtypeStruct((heads * ways, length), F32),
            jax.ShapeDtypeStruct((2, span // here, here), F32),
        ),
        in_specs=[SMEM, VMEM] + [VMEM] * chips,
        out_specs=(VMEM,) * 4,
        scratch_shapes=[pltpu.VMEM((ways, 2 * length, here), BF16)],
        compiler_params=PARAMS,
        name="state",
    )(place, mine, *kv_parts)
    pattern = others.reshape(2, span)[:, : block_pattern.size].reshape(blocks, picks).astype(jnp.int32)
    window = jnp.where(pattern >= 0, pattern - (level - 1) * blocks, 0)
    bias = jnp.repeat(jnp.where(pattern >= 0, 0.0, -1e30).astype(F32), BLK, axis=1)
    states = [onward(sent, steps) for steps in range(1, groups)]
    raw, queries = pl.pallas_call(
        lambda *refs: inside_kernel(chips, *refs),
        out_shape=(
            jax.ShapeDtypeStruct((ways, length, here), F32),
            jax.ShapeDtypeStruct((ways, length, here), BF16),
        ),
        in_specs=[SMEM, VMEM, VMEM] + [VMEM] * (2 * chips),
        out_specs=(VMEM, VMEM),
        scratch_shapes=[pltpu.VMEM((ways, 2 * length, here), BF16)],
        compiler_params=PARAMS,
        cost_estimate=pl.CostEstimate(flops=2**31, bytes_accessed=6 * 2**20, transcendentals=2**19),
        name="inside",
    )(place, decays, starts, *q_parts, *kv_parts)
    _, sparse_queries = exchange(sparse_query, after=(raw, *states))
    firsts = pl.pallas_call(
        first_kernel,
        out_shape=[pltpu.HBM((ways, length, here // 2), BF16)] * 2,
        in_specs=[VMEM] * (4 + len(states)) + [ANY],
        out_specs=[HBM] * 2,
        scratch_shapes=[pltpu.VMEM((2, ways, length, here // 2), BF16), pltpu.SemaphoreType.DMA((2,))],
        compiler_params=PARAMS,
        name="first",
    )(raw, queries, decays, gain, *states, earlier_keys)
    earlier_firsts = [onward(x) for x in firsts]

    steps = blocks // STEP
    rows = STEP * BLK
    whole = pl.BlockSpec((tokens, here), lambda g: (0, 0))
    part = pl.BlockSpec((rows, here), lambda g: (g, 0))
    table = pl.BlockSpec((heads, rows, picks * BLK), lambda g: (0, g, 0))
    weights = pl.pallas_call(
        weights_kernel,
        out_shape=jax.ShapeDtypeStruct((heads, tokens, picks * BLK), BF16),
        grid=(steps,),
        in_specs=[SMEM, whole, whole, pl.BlockSpec((blocks, picks * BLK), lambda g: (0, 0)), part],
        out_specs=table,
        scratch_shapes=[
            pltpu.VMEM((2 * tokens, here), BF16),
            pltpu.VMEM((STEP, picks * BLK, here), BF16),
        ],
        compiler_params=PARAMS,
        cost_estimate=pl.CostEstimate(flops=2**31, bytes_accessed=8 * 2**20, transcendentals=2**21),
        name="weights",
    )(
        window,
        sparse_keys.reshape(tokens, here),
        earlier_keys.reshape(tokens, here),
        bias,
        sparse_queries.reshape(tokens, here),
    )
    order = (peers[:, None] * 2 + cores[None, :]).reshape(-1).astype(jnp.int32)
    some = here // 2
    whole = pl.BlockSpec((tokens, some), lambda g, *_: (0, 0))
    sums = []
    for half, (own, earlier) in enumerate(zip(firsts, earlier_firsts)):
        outs = pl.pallas_call(
            sum_kernel,
            out_shape=[jax.ShapeDtypeStruct((2, length, some), BF16)] * chips,
            grid_spec=pltpu.PrefetchScalarGridSpec(
                num_scalar_prefetch=2,
                grid=(ways,),
                in_specs=[
                    pl.BlockSpec((heads // 2, length, picks * BLK), lambda g, order, _, half=half: (half, order[g], 0)),
                    whole,
                    whole,
                ],
                out_specs=[
                    pl.BlockSpec((1, length, some), lambda g, *_, k=k: (jnp.clip(g - 2 * k, 0, 1), 0, 0))
                    for k in range(chips)
                ],
                scratch_shapes=[
                    pltpu.VMEM((2 * tokens, some), BF16),
                    pltpu.VMEM((length // BLK, picks * BLK, some), BF16),
                ],
            ),
            compiler_params=PARAMS,
            name="sum",
        )(order, window, weights, own.reshape(tokens, some), earlier.reshape(tokens, some))
        for k, out in enumerate(outs):
            if k:
                out = lax.ppermute(out, ("side", "inner"), [(i, i ^ (2 * k)) for i in range(ways)])
            sums += [out, swap(out)]
    return pl.pallas_call(
        join_kernel,
        out_shape=jax.ShapeDtypeStruct((length, model), BF16),
        grid=(1,),
        in_specs=[SMEM]
        + [pl.BlockSpec((1, length, some), lambda g, core=n % 2: (core, 0, 0)) for n in range(len(sums))],
        out_specs=pl.BlockSpec((length, model), lambda g: (0, 0)),
        compiler_params=PARAMS,
        name="join",
    )(columns, *sums)


def solution(mesh):
    spans, inner = mesh.devices.shape
    finer = Mesh(mesh.devices.reshape(spans // 2, 2, inner), ("group", "side", "inner"))
    rows = P(("group", "side", "inner"), None)
    placed = (rows,) * 5 + (P("inner", ("group", "side")), P("inner", None), P(("group", "side"), None))
    return jax.shard_map(local, mesh=finer, in_specs=placed, out_specs=rows, check_vma=False)
```

```python
import math

import jax
import jax.numpy as jnp
from jax import lax
from jax.experimental import pallas as pl
from jax.experimental.pallas import tpu as pltpu
from jax.sharding import Mesh
from jax.sharding import PartitionSpec as P

BLK = 64
STEP = 4
F32 = jnp.float32
BF16 = jnp.bfloat16
HIGHEST = lax.Precision.HIGHEST
VMEM = pl.BlockSpec(memory_space=pltpu.VMEM)
SMEM = pl.BlockSpec(memory_space=pltpu.SMEM)
ANY = pl.BlockSpec(memory_space=pl.ANY)
HBM = pl.BlockSpec(memory_space=pltpu.HBM)
PARAMS = pltpu.CompilerParams(vmem_limit_bytes=16 * 2**20)


def halves(x):
    high = x.astype(BF16)
    return high, (x - high.astype(F32)).astype(BF16)


def dot(a, b, dims):
    return lax.dot_general(a, b, (dims, ((), ())), preferred_element_type=F32)


def exact(a, b, dims):
    return lax.dot_general(a, b, (dims, ((), ())), precision=HIGHEST, preferred_element_type=F32)


def grid_of(shape):
    return lax.broadcasted_iota(jnp.int32, shape, 0), lax.broadcasted_iota(jnp.int32, shape, 1)


def summed_down(logs):
    length = logs.shape[1]
    row, col = grid_of((length, length))
    return exact((row >= col).astype(F32), logs, ((1,), (1,)))


def other_chunks(totals, chunks, later):
    count = totals.shape[1]
    row, col = grid_of((count, count))
    same = row // chunks == col // chunks
    taken = same & ((row > col) if later else (row < col))
    return exact(totals, taken.astype(F32), ((1,), (0,)))


def run_all(copies):
    for copy in copies:
        copy.start()
    for copy in copies:
        copy.wait()


def pieces_kernel(in_ref, *refs):
    out_ref, sem = refs[-2:]
    ways, _, here = out_ref.shape
    run_all([
        pltpu.make_async_copy(
            in_ref.at[:, pl.ds((d % (ways // 2) * 2 + d // (ways // 2)) * here, here)], out_ref.at[d], sem.at[d]
        )
        for d in range(ways)
    ])


def outward_kernel(count, columns_ref, *refs):
    ins, out_ref, sem = refs[:count], refs[-2], refs[-1]
    length, here = ins[0].shape[0], out_ref.shape[2]
    run_all([
        pltpu.make_async_copy(
            ref.at[:, pl.ds(pl.multiple_of(columns_ref[k, 1], 128), here)],
            out_ref.at[k, pl.ds(n * length, length), :],
            sem.at[k, n],
        )
        for k in range(out_ref.shape[0])
        for n, ref in enumerate(ins)
    ])


def thirds(x):
    first = x.astype(BF16).astype(F32)
    second = (x - first).astype(BF16).astype(F32)
    return first, second, x - first - second


def parcel_kernel(count, extra, columns_ref, place_ref, *refs):
    ins, got_ref, table_ref = refs[:count], refs[count], refs[count + 1]
    scratch = 2 if extra else 1
    chips = got_ref.shape[0]
    outs, sem = refs[-scratch - chips : -scratch], refs[-1]
    length, here = ins[0].shape[0], got_ref.shape[2]
    core = place_ref[1]
    copies = []
    for k, out_ref in enumerate(outs):
        start = pl.multiple_of(columns_ref[k, 0], 128)
        for n, ref in enumerate(ins):
            copies.append(
                pltpu.make_async_copy(
                    ref.at[:, pl.ds(start, here)], out_ref.at[core, pl.ds(n * length, length), :], sem.at[k, n]
                )
            )
        copies.append(
            pltpu.make_async_copy(
                got_ref.at[k], out_ref.at[1 - core, pl.ds(0, count * length), :], sem.at[k, count]
            )
        )
    if extra:
        rows_ref = refs[-2]
        parts = jnp.concatenate(thirds(table_ref[...]), 0)
        if extra > parts.shape[0]:
            parts = jnp.concatenate([parts, jnp.zeros((extra - parts.shape[0], here), F32)], 0)
        for n in range(2):
            rows_ref[n] = parts.astype(BF16)
        copies.append(
            pltpu.make_async_copy(
                rows_ref, outs[chips // 2].at[:, pl.ds(count * length, extra), :], sem.at[0, count + 1]
            )
        )
    run_all(copies)


def gather_chunks(place_ref, refs, out_ref):
    for k, ref in enumerate(refs):
        chip = jnp.bitwise_xor(place_ref[0], k)
        out_ref[pl.ds(pl.multiple_of(2 * chip, 2), 2)] = ref[:, : out_ref.shape[1], :]


def state_kernel(place_ref, table_ref, *refs):
    parts, (sent_ref, start_ref, decay_ref, other_ref, kv_ref) = refs[:-5], refs[-5:]
    heads, width = sent_ref.shape[0], sent_ref.shape[2]
    chunks = kv_ref.shape[0]
    length = kv_ref.shape[1] // 2
    gather_chunks(place_ref, parts, kv_ref)
    size, here = table_ref.shape
    got = parts[len(parts) // 2][0, 2 * length :, :].astype(F32)
    mine, theirs = table_ref[...], got[:size] + got[size : 2 * size] + got[2 * size : 3 * size]
    leads = place_ref[2] == 0
    spans = (jnp.where(leads, mine, theirs), jnp.where(leads, theirs, mine))
    span = size * here // (heads + 1)
    for n, table in enumerate(spans):
        for h in range(heads):
            for t in range(chunks // 2):
                row, lane = divmod(h * span + t * length, here)
                at = h * chunks + n * (chunks // 2) + t
                decay_ref[at : at + 1, :] = table[row : row + 1, lane : lane + length]
        other_ref[n] = table[size - span // here :, :]
    down = summed_down(jnp.log(decay_ref[...]))
    totals = down[length - 1 : length, :]
    left = jnp.exp(totals - down)
    kept = jnp.exp(totals)
    factors = jnp.exp(totals + other_chunks(totals, chunks, True))
    place = lax.broadcasted_iota(jnp.int32, (16, width), 0)
    for h in range(heads):
        columns = slice(h * width, (h + 1) * width)
        state = jnp.zeros((width, width), F32)
        for c in range(chunks):
            at = h * chunks + c
            if c:
                high, low = halves(state)
                start_ref[h, c, :width, :] = high
                start_ref[h, c, width:, :] = low
            keys = kv_ref[c, :length, columns].astype(F32)
            values = kv_ref[c, length:, columns]
            high, low = halves(keys * left[:, at : at + 1])
            state = kept[:, at : at + 1] * state + dot(
                jnp.concatenate([high, low], 0), jnp.concatenate([values, values], 0), ((0,), (0,))
            )
        sent_ref[h, :width, :] = state.astype(BF16)
        factor = factors[:, h * chunks : h * chunks + 1]
        first, second, third = thirds(factor)
        sent_ref[h, width:, :] = jnp.where(
            place == 0, first, jnp.where(place == 1, second, jnp.where(place == 2, third, 0.0))
        ).astype(BF16)


def inside_kernel(count, place_ref, decay_ref, start_ref, *refs):
    q_parts, kv_parts = refs[:count], refs[count : 2 * count]
    raw_ref, out_ref, q_ref, kv_ref, sem = refs[2 * count :]
    chunks, length, here = q_ref.shape
    heads = decay_ref.shape[0] // chunks
    width = here // heads
    gather_chunks(place_ref, q_parts, q_ref)
    copy = pltpu.make_async_copy(q_ref, out_ref, sem)
    copy.start()
    gather_chunks(place_ref, kv_parts, kv_ref)
    logs = jnp.log(decay_ref[...])
    row, col = grid_of((length, length))
    along = exact(logs, (row <= col).astype(F32), ((1,), (0,)))
    down = summed_down(logs)
    lifts = jnp.exp(down)
    causal = row >= col
    for h in range(heads):
        columns = slice(h * width, (h + 1) * width)
        for c in range(chunks):
            at = h * chunks + c
            queries = q_ref[c, :, columns]
            keys = kv_ref[c, :length, columns]
            values = kv_ref[c, length:, columns]
            gap = jnp.where(causal, down[:, at : at + 1] - along[at : at + 1, :], 0.0)
            weights = jnp.where(causal, jnp.exp(gap), 0.0) * dot(queries, keys, ((1,), (1,)))
            raw = dot(jnp.concatenate(halves(weights), 1), jnp.concatenate([values, values], 0), ((1,), (0,)))
            if c:
                raw = raw + lifts[:, at : at + 1] * dot(
                    jnp.concatenate([queries, queries], 1), start_ref[h, c], ((1,), (0,))
                )
            raw_ref[c, :, columns] = raw
    copy.wait()


def first_kernel(raw_ref, q_ref, decay_ref, gain_ref, *refs):
    earlier, outs, (made_ref, sem) = refs[:-5], refs[-4:-2], refs[-2:]
    chunks, length, here = q_ref.shape
    heads, width = gain_ref.shape
    down = summed_down(jnp.log(decay_ref[...]))
    lifts = jnp.exp(down + other_chunks(down[length - 1 : length, :], chunks, False))
    copies = []
    for h in range(heads):
        columns = slice(h * width, (h + 1) * width)
        carried = jnp.zeros((width, width), F32)
        factor = jnp.ones((1, 1), F32)
        for ref in earlier:
            carried = carried + factor * ref[h, :width, :].astype(F32)
            parts = ref[h, width:, :].astype(F32)
            factor = factor * (parts[0:1, 0:1] + parts[1:2, 0:1] + parts[2:3, 0:1])
        both = jnp.concatenate(halves(carried), 0)
        gain = gain_ref[h : h + 1, :]
        half, place = divmod(h, heads // 2)
        for c in range(chunks):
            at = h * chunks + c
            queries = q_ref[c, :, columns]
            outside = dot(jnp.concatenate([queries, queries], 1), both, ((1,), (0,)))
            raw = raw_ref[c, :, columns] + lifts[:, at : at + 1] * outside
            scale = lax.rsqrt(jnp.mean(raw * raw, axis=-1, keepdims=True) + 1e-06)
            made_ref[half, c, :, place * width : (place + 1) * width] = (raw * scale * gain).astype(BF16)
        if place == heads // 2 - 1:
            copies.append(pltpu.make_async_copy(made_ref.at[half], outs[half], sem.at[half]))
            copies[-1].start()
    for copy in copies:
        copy.wait()


def pick(window_ref, b, source_ref, picked_ref):
    for j in range(picked_ref.shape[0] // BLK):
        start = pl.multiple_of(window_ref[b, j] * BLK, BLK)
        picked_ref[j * BLK : (j + 1) * BLK, :] = source_ref[pl.ds(start, BLK), :]


def weights_kernel(window_ref, own_ref, earlier_ref, bias_ref, q_ref, out_ref, keys_ref, picked_ref):
    tokens, here = own_ref.shape
    heads = out_ref.shape[0]
    width = here // heads
    picks = picked_ref.shape[1] // BLK
    group = pl.program_id(0)

    @pl.when(group == 0)
    def _():
        keys_ref[:tokens, :] = earlier_ref[...]
        keys_ref[tokens:, :] = own_ref[...]

    row, col = grid_of((BLK, picks * BLK))
    causal = jnp.where((col >= BLK) | (col <= row), 0.0, -1e30)
    scale = 1.0 / math.sqrt(width)
    for t in range(STEP):
        b = group * STEP + t
        pick(window_ref, b, keys_ref, picked_ref.at[t])
        bias = causal + bias_ref[pl.ds(b, 1), :]
        for h in range(heads):
            columns = slice(h * width, (h + 1) * width)
            scores = dot(q_ref[t * BLK : (t + 1) * BLK, columns], picked_ref[t, :, columns], ((1,), (1,))) * scale
            scores = scores + bias
            probs = jnp.exp(scores - jnp.max(scores, axis=-1, keepdims=True))
            share = 1.0 / jnp.sum(probs, axis=-1, keepdims=True)
            out_ref[h, t * BLK : (t + 1) * BLK, :] = (probs * share).astype(BF16)


def sum_kernel(order_ref, window_ref, weights_ref, own_ref, earlier_ref, *refs):
    outs, values_ref, picked_ref = refs[:-2], refs[-2], refs[-1]
    tokens, here = own_ref.shape
    heads, length, _ = weights_ref.shape
    width = here // heads
    step = pl.program_id(0)

    @pl.when(step == 0)
    def _():
        values_ref[:tokens, :] = earlier_ref[...]
        values_ref[tokens:, :] = own_ref[...]

    results = []
    for t in range(length // BLK):
        b = order_ref[step] * (length // BLK) + t
        pick(window_ref, b, values_ref, picked_ref.at[t])
        rows = pl.ds(pl.multiple_of(b * BLK, BLK), BLK)
        for h in range(heads):
            columns = slice(h * width, (h + 1) * width)
            second = dot(weights_ref[h, t * BLK : (t + 1) * BLK, :], picked_ref[t, :, columns], ((1,), (0,)))
            results.append((t, columns, (own_ref[rows, columns].astype(F32) + second).astype(BF16)))
    for k, out_ref in enumerate(outs):

        @pl.when(step // 2 == k)
        def _(out_ref=out_ref):
            for t, columns, result in results:
                out_ref[0, t * BLK : (t + 1) * BLK, columns] = result


def join_kernel(columns_ref, *refs):
    parts, out_ref = refs[:-1], refs[-1]
    here = parts[0].shape[2]
    chips = columns_ref.shape[0]
    for n, ref in enumerate(parts):
        half, k, core = n // (2 * chips), n // 2 % chips, n % 2
        start = pl.multiple_of(columns_ref[k, core] + half * here, 128)
        out_ref[:, pl.ds(start, here)] = ref[0]


def local(lin_query, lin_key, lin_value, sparse_query, sparse_key, decay, norm_gain, block_pattern):
    groups, inner = lax.axis_size("group"), lax.axis_size("inner")
    level, side, index = lax.axis_index("group"), lax.axis_index("side"), lax.axis_index("inner")
    ways = 2 * inner
    chips = ways // 2
    length, model = lin_query.shape
    width = norm_gain.shape[1]
    heads = norm_gain.shape[0] // 2
    here = heads * width
    tokens = ways * length
    blocks = tokens // BLK
    picks = block_pattern.shape[1]

    chip, core = side * (inner // 2) + index // 2, index % 2
    place = jnp.stack([chip, core, side]).astype(jnp.int32)
    peers = jnp.bitwise_xor(chip, jnp.arange(chips, dtype=jnp.int32))
    cores = jnp.stack([core, 1 - core])
    indices = (peers % (inner // 2))[:, None] * 2 + cores[None, :]
    columns = ((indices * 2 + (peers // (inner // 2))[:, None]) * here).astype(jnp.int32)

    def swap(x):
        return lax.ppermute(x, ("side", "inner"), [(i, i ^ 1) for i in range(ways)])

    def spread(*arrays, table=None, after=(), first=()):
        rows = len(arrays) * length
        extra = 0 if table is None else -(-3 * table.shape[0] // 16) * 16
        after = after if table is None else (table, *after)
        out = pl.pallas_call(
            lambda *refs: outward_kernel(len(arrays), *refs),
            out_shape=pltpu.HBM((chips, rows, here), BF16),
            in_specs=[SMEM] + [VMEM] * len(arrays) + [ANY] * len(first),
            out_specs=HBM,
            scratch_shapes=[pltpu.SemaphoreType.DMA((chips, len(arrays)))],
            compiler_params=PARAMS,
            name="outward",
        )(columns, *arrays, *first)
        parcels = pl.pallas_call(
            lambda *refs: parcel_kernel(len(arrays), extra, *refs),
            out_shape=[
                pltpu.HBM((2, rows + (extra if k == chips // 2 else 0), here), BF16) for k in range(chips)
            ],
            in_specs=[SMEM, SMEM] + [VMEM] * (len(arrays) + 1) + [VMEM] * bool(extra) + [ANY] * (len(after) - bool(extra)),
            out_specs=[HBM] * chips,
            scratch_shapes=[pltpu.VMEM((2, extra, here), BF16)] * bool(extra)
            + [pltpu.SemaphoreType.DMA((chips, len(arrays) + 2))],
            compiler_params=PARAMS,
            name="parcels",
        )(columns, place, *arrays, swap(out), *after)
        return parcels, [parcels[0]] + [
            lax.ppermute(x, ("side", "inner"), [(i, i ^ (2 * k)) for i in range(ways)])
            for k, x in enumerate(parcels)
            if k
        ]

    def exchange(x, after=()):
        pieces = pl.pallas_call(
            pieces_kernel,
            out_shape=pltpu.HBM((ways, length, here), BF16),
            in_specs=[VMEM] + [ANY] * len(after),
            out_specs=HBM,
            scratch_shapes=[pltpu.SemaphoreType.DMA((ways,))],
            compiler_params=PARAMS,
            name="pieces",
        )(x, *after)
        return pieces, lax.all_to_all(pieces, ("side", "inner"), split_axis=0, concat_axis=0, tiled=True)

    def onward(x, steps=1):
        return lax.ppermute(x, "group", [(i, i + steps) for i in range(groups - steps)])

    span = decay.shape[1]
    flat = block_pattern.reshape(1, -1).astype(F32)
    flat = jnp.pad(flat, ((0, 0), (0, span - flat.shape[1])))

    def table(first_head):
        return jnp.concatenate([lax.dynamic_slice_in_dim(decay, first_head, heads, 0), flat], 0).reshape(-1, here)

    mine = table(side * heads)
    gain = lax.dynamic_slice_in_dim(norm_gain, side * heads, heads, 0)

    pieces, sparse_keys = exchange(sparse_key)
    parcels, kv_parts = spread(lin_key, lin_value, table=table((1 - side) * heads), first=(pieces,))
    _, q_parts = spread(lin_query, after=kv_parts[1:3])
    earlier_keys = onward(sparse_keys)

    sent, starts, decays, others = pl.pallas_call(
        state_kernel,
        out_shape=(
            jax.ShapeDtypeStruct((heads, width + 16, width), BF16),
            jax.ShapeDtypeStruct((heads, ways, 2 * width, width), BF16),
            jax.ShapeDtypeStruct((heads * ways, length), F32),
            jax.ShapeDtypeStruct((2, span // here, here), F32),
        ),
        in_specs=[SMEM, VMEM] + [VMEM] * chips,
        out_specs=(VMEM,) * 4,
        scratch_shapes=[pltpu.VMEM((ways, 2 * length, here), BF16)],
        compiler_params=PARAMS,
        name="state",
    )(place, mine, *kv_parts)
    pattern = others.reshape(2, span)[:, : block_pattern.size].reshape(blocks, picks).astype(jnp.int32)
    window = jnp.where(pattern >= 0, pattern - (level - 1) * blocks, 0)
    bias = jnp.repeat(jnp.where(pattern >= 0, 0.0, -1e30).astype(F32), BLK, axis=1)
    states = [onward(sent, steps) for steps in range(1, groups)]
    raw, queries = pl.pallas_call(
        lambda *refs: inside_kernel(chips, *refs),
        out_shape=(
            jax.ShapeDtypeStruct((ways, length, here), F32),
            pltpu.HBM((ways, length, here), BF16),
        ),
        in_specs=[SMEM, VMEM, VMEM] + [VMEM] * (2 * chips),
        out_specs=(VMEM, HBM),
        scratch_shapes=[
            pltpu.VMEM((ways, length, here), BF16),
            pltpu.VMEM((ways, 2 * length, here), BF16),
            pltpu.SemaphoreType.DMA,
        ],
        compiler_params=PARAMS,
        cost_estimate=pl.CostEstimate(flops=2**31, bytes_accessed=6 * 2**20, transcendentals=2**19),
        name="inside",
    )(place, decays, starts, *q_parts, *kv_parts)
    _, sparse_queries = exchange(sparse_query, after=(raw, *states))
    firsts = pl.pallas_call(
        first_kernel,
        out_shape=[pltpu.HBM((ways, length, here // 2), BF16)] * 2,
        in_specs=[VMEM] * (4 + len(states)) + [ANY],
        out_specs=[HBM] * 2,
        scratch_shapes=[pltpu.VMEM((2, ways, length, here // 2), BF16), pltpu.SemaphoreType.DMA((2,))],
        compiler_params=PARAMS,
        name="first",
    )(raw, queries, decays, gain, *states, earlier_keys)
    earlier_firsts = [onward(x) for x in firsts]

    steps = blocks // STEP
    rows = STEP * BLK
    whole = pl.BlockSpec((tokens, here), lambda g: (0, 0))
    part = pl.BlockSpec((rows, here), lambda g: (g, 0))
    table = pl.BlockSpec((heads, rows, picks * BLK), lambda g: (0, g, 0))
    weights = pl.pallas_call(
        weights_kernel,
        out_shape=jax.ShapeDtypeStruct((heads, tokens, picks * BLK), BF16),
        grid=(steps,),
        in_specs=[SMEM, whole, whole, pl.BlockSpec((blocks, picks * BLK), lambda g: (0, 0)), part],
        out_specs=table,
        scratch_shapes=[
            pltpu.VMEM((2 * tokens, here), BF16),
            pltpu.VMEM((STEP, picks * BLK, here), BF16),
        ],
        compiler_params=PARAMS,
        cost_estimate=pl.CostEstimate(flops=2**31, bytes_accessed=8 * 2**20, transcendentals=2**21),
        name="weights",
    )(
        window,
        sparse_keys.reshape(tokens, here),
        earlier_keys.reshape(tokens, here),
        bias,
        sparse_queries.reshape(tokens, here),
    )
    order = (peers[:, None] * 2 + cores[None, :]).reshape(-1).astype(jnp.int32)
    some = here // 2
    whole = pl.BlockSpec((tokens, some), lambda g, *_: (0, 0))
    sums = []
    for half, (own, earlier) in enumerate(zip(firsts, earlier_firsts)):
        outs = pl.pallas_call(
            sum_kernel,
            out_shape=[jax.ShapeDtypeStruct((2, length, some), BF16)] * chips,
            grid_spec=pltpu.PrefetchScalarGridSpec(
                num_scalar_prefetch=2,
                grid=(ways,),
                in_specs=[
                    pl.BlockSpec((heads // 2, length, picks * BLK), lambda g, order, _, half=half: (half, order[g], 0)),
                    whole,
                    whole,
                ],
                out_specs=[
                    pl.BlockSpec((1, length, some), lambda g, *_, k=k: (jnp.clip(g - 2 * k, 0, 1), 0, 0))
                    for k in range(chips)
                ],
                scratch_shapes=[
                    pltpu.VMEM((2 * tokens, some), BF16),
                    pltpu.VMEM((length // BLK, picks * BLK, some), BF16),
                ],
            ),
            compiler_params=PARAMS,
            name="sum",
        )(order, window, weights, own.reshape(tokens, some), earlier.reshape(tokens, some))
        for k, out in enumerate(outs):
            if k:
                out = lax.ppermute(out, ("side", "inner"), [(i, i ^ (2 * k)) for i in range(ways)])
            sums += [out, swap(out)]
    return pl.pallas_call(
        join_kernel,
        out_shape=jax.ShapeDtypeStruct((length, model), BF16),
        grid=(1,),
        in_specs=[SMEM]
        + [pl.BlockSpec((1, length, some), lambda g, core=n % 2: (core, 0, 0)) for n in range(len(sums))],
        out_specs=pl.BlockSpec((length, model), lambda g: (0, 0)),
        compiler_params=PARAMS,
        name="join",
    )(columns, *sums)


def solution(mesh):
    spans, inner = mesh.devices.shape
    finer = Mesh(mesh.devices.reshape(spans // 2, 2, inner), ("group", "side", "inner"))
    rows = P(("group", "side", "inner"), None)
    placed = (rows,) * 5 + (P("inner", ("group", "side")), P("inner", None), P(("group", "side"), None))
    return jax.shard_map(local, mesh=finer, in_specs=placed, out_specs=rows, check_vma=False)
```
